512 devices in a mesh: grp: 2 (over core), ep: 128 (over z_lo, x, y), tp: 2 (over z_hi).
Axes of the slice: x: 4, y: 8, z: 8 (z_hi: 2, z_lo: 4; z = z_hi * 4 + z_lo), core: 2. Of those that a mesh axis runs over, the one named last changes fastest.
Arguments:
- master: float32 [2048, 128, 768], P(('grp', 'ep'), None, 'tp'), may hold values from -0.21875 to 0.21875
- gate_up: bfloat16 [128, 2, 2048, 768], P('ep', None, 'grp', 'tp'), may hold values from -0.125 to 0.125
- owner_map: int32 [128], replicated, may hold values from 0 to 127, each once
- tokens: bfloat16 [4, 2048, 2048], P(None, 'ep', 'grp'), may hold values from -6 to 6
- routes: int32 [4, 2048, 8], P(None, 'ep'), may hold values from 0 to 127, all different within a row; in each aligned block of 16 rows (0 to 15, 16 to 31, ..., all dimensions but the last counted through in order) at most 2 rows name the same one
- gate_weights: float32 [4, 2048, 8], P(None, 'ep'), may hold values from 0.1 to 1
Outputs:
- mixed: bfloat16 [4, 2048, 2048], P(None, 'ep', 'grp')
The draws below stay inside these ranges and needn't reach their ends.
Inputs may be any that keep to these rules, and one draw needn't show every extreme that they name: `owner_map`: each owner index appears exactly once. `routes`: within the rows of one device of one step (aligned blocks of 16 rows) no expert is named by more than 2 rows, a bound that some block reaches in every draw.
All inputs are finite; a program needn't handle non-finite values.
Results may differ from the reference program's by a relative error of at most 0.0049.
Values may be sent and summed in bfloat16 or wider, within the bound.
A program may use at most 64 MiB of HBM per device.

```python
import math
import jax
import jax.numpy as jnp
import numpy as np
from jax import lax

D = 2048
FF = 768
TOPK = 8
QB = 128
STEPS = 4
ROWS_DEV = 16
EXPERTS = 128
ROWS = 2048
CAP = 2
N_EP = 128


def levels(rng, shape, cuts, least, high):
    def one(axis_at, shards_of):
        heights = jax.random.uniform(jax.random.fold_in(jax.random.fold_in(rng, 6), axis_at), (shards_of,), jnp.float32, least / len(cuts), high / len(cuts))
        return jnp.repeat(jnp.exp(heights), shape[axis_at] // shards_of).reshape((-1,) + (1,) * (len(shape) - axis_at - 1))

    factor_of = one(*cuts[0])
    for cut in cuts[1:]:
        factor_of = factor_of * one(*cut)
    return factor_of


def shared_out(rng, own, number, rows, amount, top, reach, skew):
    sequence = jax.random.permutation(rng, amount)
    packed, ordinary = load_shares(amount, rows * top, reach, skew, True), load_shares(amount, rows * top, reach, skew, False)
    places = jnp.arange(amount)

    def named(tallies, turn):
        used = int((tallies > 0).sum())
        fixed = max(1, used // 4)
        shifted = fixed + (places - fixed + turn * (used - fixed)) % max(1, amount - fixed)
        return jnp.zeros((amount,), jnp.int32).at[sequence[jnp.where(places < fixed, places, shifted)]].set(jnp.asarray(tallies, jnp.int32))

    tallies = jnp.where(number % 4 == 0, named(packed, number // 4), named(ordinary, number - number // 4 - 1))
    mixed = jax.random.permutation(jax.random.fold_in(own, 3), amount)
    donor, sink = mixed[0:amount // 2 * 2:2], mixed[1:amount // 2 * 2:2]
    room = jnp.minimum(tallies[donor] - 1, reach - tallies[sink]) // 2
    room = jnp.where((donor == sequence[0]) | (sink == sequence[0]) | (tallies[sink] == 0), 0, jnp.maximum(room, 0))
    shifted = jax.random.randint(jax.random.fold_in(own, 4), (amount // 2,), 0, 1 << 20) % (room + 1)
    tallies = tallies.at[donor].add(-shifted).at[sink].add(shifted)
    labels = jnp.searchsorted(jnp.cumsum(tallies), jnp.arange(rows * top), side="right").astype(jnp.int32)
    grid = labels.reshape(top, rows).T
    grid = grid[jax.random.permutation(jax.random.fold_in(own, 1), rows)]
    turn = jax.random.randint(jax.random.fold_in(own, 2), (rows, 1), 0, top)
    return jnp.take_along_axis(grid, (jnp.arange(top)[None, :] + turn) % top, axis=1)


def load_shares(amount, total, limit, slope, full):
    portions = [(1 << 20) // math.isqrt(grade ** slope) + 1 for grade in range(1, amount + 1)]
    largest = limit if full else min(limit, max(-(-total // amount), total * portions[0] // sum(portions)))
    least = 1 if total - largest >= amount - 1 else 0
    given, spare = [largest] + [least] * (amount - 1), total - largest - least * (amount - 1)
    while spare > 0:
        free = [i for i in range(1, amount) if given[i] < largest] or [i for i in range(1, amount) if given[i] < limit]
        mass, remaining = sum([portions[i] for i in free]), spare
        for i in free:
            addition = min(limit - given[i], max(1, remaining * portions[i] // mass), spare)
            given[i] = given[i] + addition
            spare = spare - addition
    return np.array(given)


def gaussian(key, shape, width, most, shards=(), kind=jnp.bfloat16):
    values = jax.random.normal(key, shape, jnp.float32) * width
    if len(shards) > 0:
        values = levels(key, shape, shards, -0.22, 0.18) * values
    return jnp.clip(values, min=-most, max=most).astype(kind)


def setup_inputs(seed: int = 0) -> dict:
    key_of = jax.random.split(jax.random.key(seed), 7)
    master = gaussian(key_of[0], (D, EXPERTS, FF), FF ** -0.5, 0.21875, ((0, 256), (2, 2)), jnp.float32)
    gate_up = gaussian(key_of[1], (EXPERTS, 2, D, FF), D ** -0.5, 0.125, ((0, 128), (2, 2), (3, 2)))
    owner_map = jax.random.permutation(key_of[2], EXPERTS).astype(jnp.int32)
    tokens = gaussian(key_of[3], (STEPS, ROWS, D), 1.0, 6.0, ((1, 128), (2, 2)))
    routes_keys = jax.random.split(jax.random.fold_in(key_of[4], 1), STEPS * ROWS // ROWS_DEV)
    routes_turns = jax.random.permutation(jax.random.fold_in(key_of[4], 3), STEPS * ROWS // ROWS_DEV)
    routes = jax.vmap(lambda own, number: shared_out(jax.random.fold_in(key_of[4], 2), own, number, ROWS_DEV, EXPERTS, TOPK, CAP, 2))(routes_keys, routes_turns).reshape((STEPS, ROWS, TOPK))
    gate_weights = jnp.clip(0.1 + 0.9 * jax.random.uniform(key_of[5], (STEPS, ROWS, TOPK), jnp.float32) ** levels(key_of[5], (STEPS, ROWS, TOPK), ((1, 128),), -0.2, 0.2), 0.1, 1.0)
    return {"master": master, "gate_up": gate_up, "owner_map": owner_map, "tokens": tokens, "routes": routes, "gate_weights": gate_weights}


def float_grid(values):
    magnitude = jnp.abs(values)
    spacing = jnp.full_like(magnitude, 2.0 ** -9)
    for exponent in range(-5, 9):
        spacing = jnp.where(magnitude >= 2.0 ** exponent, 2.0 ** (exponent - 3), spacing)
    snapped = jnp.floor(magnitude / spacing + 0.5) * spacing
    return jnp.where(values < 0, -snapped, snapped)


def reference(master, gate_up, owner_map, tokens, routes, gate_weights):
    nrow = D // QB
    ncol = FF // QB
    slots = N_EP * CAP
    amax = jnp.max(jnp.abs(master).reshape(nrow, QB, EXPERTS, ncol, QB), axis=(1, 4))
    scales = (amax + 1e-6) / 448.0

    def code_expert(expert):
        field = lax.dynamic_index_in_dim(master, expert, 1, keepdims=False)
        block_scale = lax.dynamic_index_in_dim(scales, expert, 1, keepdims=False)
        full_scale = jnp.repeat(jnp.repeat(block_scale, QB, axis=0), QB, axis=1)
        return float_grid(field / full_scale).astype(jnp.bfloat16)

    code_table = lax.map(code_expert, jnp.arange(EXPERTS, dtype=jnp.int32))
    outputs = []
    for step in range(STEPS):
        ids_flat = routes[step].reshape(-1)
        weight_flat = gate_weights[step].reshape(-1)
        rows_now = tokens[step]

        def one_expert(mixed, expert):
            found = jnp.nonzero(ids_flat == expert, size=slots, fill_value=0)[0].astype(jnp.int32)
            count = jnp.sum((ids_flat == expert).astype(jnp.int32))
            valid = jnp.arange(slots, dtype=jnp.int32) < count
            picked = (found // TOPK).astype(jnp.int32)
            inputs = rows_now[picked]
            owner = owner_map[expert]
            weights = lax.dynamic_index_in_dim(gate_up, owner, 0, keepdims=False)
            gated = jnp.dot(inputs, weights[0], preferred_element_type=jnp.float32)
            upped = jnp.dot(inputs, weights[1], preferred_element_type=jnp.float32)
            hidden = (jax.nn.silu(gated) * upped).astype(jnp.bfloat16)
            block_scale = lax.dynamic_index_in_dim(scales, expert, 1, keepdims=False)
            codes = lax.dynamic_index_in_dim(code_table, expert, 0, keepdims=False)
            parts = jnp.einsum("nbq,dbq->bnd", hidden.reshape(slots, ncol, QB).astype(jnp.float32),
                               codes.reshape(D, ncol, QB).astype(jnp.float32))
            column_scale = jnp.repeat(block_scale.T, QB, axis=1)
            result = jnp.sum(parts * column_scale[:, None, :], axis=0)
            weight = jnp.where(valid, weight_flat[found], jnp.float32(0.0))
            mixed = mixed.at[picked].add(result * weight[:, None])
            return mixed, None

        start = jnp.zeros((ROWS, D), jnp.float32)
        mixed, unused = lax.scan(one_expert, start, jnp.arange(EXPERTS, dtype=jnp.int32))
        outputs.append(mixed.astype(jnp.bfloat16))
    return jnp.stack(outputs)
```

```python
import functools

import jax
import jax.numpy as jnp
from jax import lax
from jax.experimental import pallas as pl
from jax.experimental.pallas import tpu as pltpu
from jax.sharding import PartitionSpec as P

f32 = jnp.float32
bf16 = jnp.bfloat16
NT = (((1,), (1,)), ((), ()))


def mm(a, b):
    return jnp.dot(a, b, preferred_element_type=f32)


def mm_nt(a, b):
    return lax.dot_general(a, b, NT, preferred_element_type=f32)


def iota(shape, dim):
    return lax.broadcasted_iota(jnp.int32, shape, dim)


def snap(values):
    magnitude = jnp.abs(values)
    spacing = jnp.full_like(magnitude, 2.0 ** (-9))
    inverse = jnp.full_like(magnitude, 2.0**9)
    for exponent in range(-5, 9):
        above = magnitude >= 2.0**exponent
        spacing = jnp.where(above, 2.0 ** (exponent - 3), spacing)
        inverse = jnp.where(above, 2.0 ** (3 - exponent), inverse)
    snapped = jnp.floor(magnitude * inverse + 0.5) * spacing
    return jnp.where(values < 0, -snapped, snapped)


def kernel(
    nz, nx, ny,
    master, gate_up, owner_map, tokens, routes, gates,
    out,
    wt, agw, ag, xs, xr, cmb, part, partr, ys, yr, rs, rr, ts, tr,
    pk, pkr, pk2, pk2r, sa, ra, sb, rb, wd, perm,
    s_ag, s_agw, s_xz, s_grp, s_ret, s_rs, s_tp, s_pk, s_pk2, s_ca, s_cb,
    r_ag, r_agw, r_xz, r_grp, r_ret, r_rs, r_tp, r_pk, r_pk2, r_ca, r_cb,
):
    steps, rows, width = tokens.shape
    experts = owner_map.shape[1]
    top = routes.shape[1]
    depth, _, hid = master.shape
    half_depth = depth // 2
    nq = nz * nx
    slots = 2 * ny
    line = ny * rows
    g = lax.axis_index("grp")
    ep = lax.axis_index("ep")
    t = lax.axis_index("tp")
    z, x, y = ep // (nx * ny), (ep // ny) % nx, ep % ny
    zz = t * nz + z

    def y_peer(dy):
        return {"ep": ep - y + (y + dy + ny) % ny}

    def ring_peer(j, sign):
        dz, dx = j // nx, j % nx
        if 2 * dz < nz:
            off = dz
        elif 2 * dz > nz:
            off = dz - nz
        else:
            off = dz * (1 - 2 * g)
        zt = (zz + sign * off + 2 * nz) % (2 * nz)
        xt = (x + sign * dx + nx) % nx
        return {"ep": (zt % nz) * (nx * ny) + xt * ny + y, "tp": zt // nz}

    def group_peer(j, sign):
        dz, dx = j // nx, j % nx
        zt = (z + sign * dz + nz) % nz
        xt = (x + sign * dx + nx) % nx
        return {"ep": zt * (nx * ny) + xt * ny + y}

    x_mate = {"ep": ep + (1 - 2 * (x % 2)) * ny}
    grp_mate = {"grp": 1 - g}
    tp_mate = {"tp": 1 - t}

    greeted = [y_peer(dy) for dy in range(1, ny)]
    greeted += [ring_peer(j, 1) for j in range(1, nq)]
    greeted += [ring_peer(j, -1) for j in range(1, nq) if 2 * (j // nx) == nz]
    greeted += [group_peer(j, 1) for j in range(nx, nq)]
    greeted += [grp_mate, tp_mate]
    barrier = pltpu.get_barrier_semaphore()
    for peer in greeted:
        pl.semaphore_signal(barrier, inc=1, device_id=peer, device_id_type=pl.DeviceIdType.MESH)

    def send(src, dst, ssem, rsem, peer):
        pltpu.make_async_remote_copy(
            src_ref=src, dst_ref=dst, send_sem=ssem, recv_sem=rsem,
            device_id=peer, device_id_type=pl.DeviceIdType.MESH,
        ).start()

    def await_bytes(ref, sem):
        pltpu.make_async_copy(ref, ref, sem).wait()

    lanes_e = iota((steps * rows, experts), 1)
    weight_of = jnp.zeros((steps * rows, experts), f32)
    for k in range(top):
        weight_of += jnp.where(routes[:, k:k + 1] == lanes_e, gates[:, k:k + 1], 0.0)
    wt[...] = weight_of.reshape(steps, rows, experts)
    pl.semaphore_wait(barrier, len(greeted))

    for dy in range(1, ny):
        send(wt, agw.at[dy], s_agw, r_agw, y_peer(dy))
    agw[0] = weight_of.reshape(steps, rows, experts)

    def gather_start(s, carry):
        for dy in range(1, ny):
            send(tokens.at[s], ag.at[s, dy], s_ag, r_ag.at[s], y_peer(dy))
        ag[s, 0] = tokens[s]
        return carry

    lax.fori_loop(0, steps, gather_start, 0)

    cols = hid // 128
    lanes_p = iota((experts, 128), 1)
    peaks = jnp.zeros((experts, 128), f32)
    for j in range(cols):
        most = jnp.abs(master[0, :, j * 128:(j + 1) * 128])
        for d in range(1, depth):
            most = jnp.maximum(most, jnp.abs(master[d, :, j * 128:(j + 1) * 128]))
        peaks = jnp.where(lanes_p == j, jnp.max(most, axis=1, keepdims=True), peaks)
    pk[...] = peaks.T[:8]
    for dy in range(1, ny):
        send(pk, pkr.at[dy], s_pk, r_pk, y_peer(dy))
    pkr[0] = pk[...]
    await_bytes(pkr.at[pl.ds(1, ny - 1)], r_pk)
    pk2[...] = jnp.max(pkr[...], axis=0)
    send(pk2, pk2r, s_pk2, r_pk2, x_mate)

    row_q = iota((nq * slots, 1), 0)
    peer_q = row_q // slots
    owner_q = (
        ((z + peer_q // nx) % nz) * (nx * ny) + ((x + peer_q % nx) % nx) * ny + y
    )
    pick = (owner_map[...] == owner_q).astype(f32).astype(bf16)
    slot_col = row_q % slots
    slot_row = iota((1, nq * slots), 1) % slots
    row_col = iota((line, 1), 0) // rows
    row_row = iota((1, line), 1) // rows
    la, lb = iota((line, line), 0), iota((line, line), 1)
    lower = ((la // rows == lb // rows) & (lb < la)).astype(f32).astype(bf16)
    spot = ((slot_col // 2) == row_row)
    spot_t = ((slot_row // 2) == row_col)
    order_col = (slot_col % 2 + 1).astype(f32)
    order_row = (slot_row % 2 + 1).astype(f32)

    await_bytes(pk2r, r_pk2)
    both = jnp.maximum(pk2[...], pk2r[...])
    scale_t = (both + 1e-06) / 448.0
    scale = jnp.concatenate([scale_t, jnp.zeros((128 - 8, experts), f32)], axis=0).T

    row_p = iota((experts, 1), 0)
    peer_p = row_p % nq
    owner_p = (
        ((z + peer_p // nx) % nz) * (nx * ny)
        + ((x + peer_p % nx) % nx) * ny
        + (y + row_p // nq) % ny
    )
    order_p = (owner_map[...] == owner_p).astype(f32).astype(bf16)

    def code(d, carry):
        for h in range(2):
            pieces = []
            for j in range(cols):
                own = scale[:, j:j + 1]
                field = master[h * half_depth + d, :, j * 128:(j + 1) * 128]
                pieces.append((snap(field / own) * own).astype(bf16))
            moved = mm(order_p, jnp.concatenate(pieces, axis=1))
            sa[:, h, :, pl.ds(pl.multiple_of(d * hid, 128), hid)] = moved.astype(bf16).reshape(ny, nq, hid)
        return carry

    lax.fori_loop(0, half_depth, code, 0)
    for dy in range(1, ny):
        send(sa.at[dy], ra.at[dy], s_ca, r_ca, y_peer(dy))
    ra[0] = sa[0]
    await_bytes(agw.at[pl.ds(1, ny - 1)], r_agw)

    def dispatch(s):
        weights = agw[:, s].reshape(line, experts)
        named = (weights > 0).astype(f32)
        ahead = mm(lower, named.astype(bf16))
        turn = (named * (ahead + 1.0)).astype(bf16)
        chosen = (mm_nt(pick, turn) == order_col) & spot
        await_bytes(ag.at[s, pl.ds(1, ny - 1)], r_ag.at[s])
        moved = mm(chosen.astype(f32).astype(bf16), ag[s].reshape(line, width))
        moved = moved.astype(bf16).reshape(nq, slots, width)
        xs[s] = moved
        for j in range(1, nq):
            send(xs.at[s, j], xr.at[s, j], s_xz, r_xz.at[s], ring_peer(j, 1))
        xr[s, 0] = xs[s, 0]
        kept = (mm_nt(turn, pick) == order_row) & spot_t
        upper = weights.astype(bf16)
        rest = (weights - upper.astype(f32)).astype(bf16)
        cmb[s, 0] = jnp.where(kept, mm_nt(upper, pick), 0.0).astype(bf16)
        cmb[s, 1] = jnp.where(kept, mm_nt(rest, pick), 0.0).astype(bf16)

    def regroup():
        a, b = iota((2 * experts, 2 * experts), 0), iota((2 * experts, 2 * experts), 1)
        j, dy, h = a // (2 * ny), (a // 2) % ny, a % 2
        order = (b == (dy * 2 + h) * nq + j).astype(f32).astype(bf16)
        await_bytes(ra.at[pl.ds(1, ny - 1)], r_ca)
        moved = mm(order, ra[...].reshape(2 * experts, half_depth * hid))
        sb[...] = moved.astype(bf16).reshape(nq, 2 * ny, half_depth * hid)
        for j in range(1, nq):
            send(sb.at[j], rb.at[j], s_cb, r_cb, group_peer(j, 1))
        rb[0] = sb[0]
        c = iota((1, 2 * experts), 1)
        j, dy, h = c // (2 * ny), (c // 2) % ny, c % 2
        source = (
            ((z - j // nx + nz) % nz) * (nx * ny) + ((x - j % nx + nx) % nx) * ny + (y - dy + ny) % ny
        )
        base = source * depth + h * half_depth
        feature = iota((width, 1), 0)
        for d in range(half_depth):
            perm[:, d * 2 * experts:(d + 1) * 2 * experts] = (feature == base + d).astype(f32).astype(bf16)

    def place():
        await_bytes(rb.at[pl.ds(1, nq - 1)], r_cb)
        total = jnp.zeros((width, hid), f32)
        for d in range(half_depth):
            total += mm(
                perm[:, d * 2 * experts:(d + 1) * 2 * experts],
                rb[:, :, d * hid:(d + 1) * hid].reshape(2 * experts, hid),
            )
        wd[...] = total.astype(bf16)

    def expert_in(s):
        await_bytes(xr.at[s, pl.ds(1, nq - 1)], r_xz.at[s])
        items = xr[s].reshape(nq * slots, width)
        part[s, 0] = mm(items, gate_up[0])
        part[s, 1] = mm(items, gate_up[1])
        send(part.at[s], partr.at[s], s_grp, r_grp.at[s], grp_mate)

    def expert_out(s):
        await_bytes(partr.at[s], r_grp.at[s])
        gated = part[s, 0] + partr[s, 0]
        upped = part[s, 1] + partr[s, 1]
        hidden = (gated / (1.0 + jnp.exp(-gated)) * upped).astype(bf16)
        result = mm_nt(hidden, wd[...])
        ys[s] = result.astype(bf16).reshape(nq, slots, width)
        for j in range(1, nq):
            send(ys.at[s, j], yr.at[s, j], s_ret, r_ret.at[s], ring_peer(j, -1))
        yr[s, 0] = ys[s, 0]

    def combine(s):
        await_bytes(yr.at[s, pl.ds(1, nq - 1)], r_ret.at[s])
        items = yr[s].reshape(nq * slots, width)
        mixed = mm(cmb[s, 0], items) + mm(cmb[s, 1], items)
        rs[s] = mixed.astype(bf16).reshape(ny, rows, width)
        for dy in range(1, ny):
            send(rs.at[s, dy], rr.at[s, dy], s_rs, r_rs.at[s], y_peer(-dy))
        rr[s, 0] = rs[s, 0]

    def total(s):
        await_bytes(rr.at[s, pl.ds(1, ny - 1)], r_rs.at[s])
        mixed = rr[s, 0].astype(f32)
        for dy in range(1, ny):
            mixed += rr[s, dy].astype(f32)
        ts[s] = mixed.astype(bf16)
        send(ts.at[s], tr.at[s], s_tp, r_tp.at[s], tp_mate)

    def turn_of(i, carry):
        @pl.when(i < steps)
        def _():
            dispatch(i)

        @pl.when(i == 0)
        def _():
            regroup()

        @pl.when((i >= 1) & (i <= steps))
        def _():
            expert_in(i - 1)

        @pl.when(i == 1)
        def _():
            place()

        @pl.when((i >= 1) & (i <= steps))
        def _():
            expert_out(i - 1)

        @pl.when((i >= 2) & (i <= steps + 1))
        def _():
            combine(i - 2)

        @pl.when(i >= 3)
        def _():
            total(i - 3)

        return carry

    lax.fori_loop(0, steps + 3, turn_of, 0)

    def finish(s, carry):
        await_bytes(tr.at[s], r_tp.at[s])
        out[s] = (ts[s].astype(f32) + tr[s].astype(f32)).astype(bf16)
        return carry

    lax.fori_loop(0, steps, finish, 0)

    rest_y, rest_q = pl.ds(1, ny - 1), pl.ds(1, nq - 1)
    await_bytes(agw.at[rest_y], s_agw)
    await_bytes(ag.at[:, rest_y], s_ag)
    await_bytes(pkr.at[rest_y], s_pk)
    await_bytes(pk2r, s_pk2)
    await_bytes(ra.at[rest_y], s_ca)
    await_bytes(rb.at[rest_q], s_cb)
    await_bytes(xr.at[:, rest_q], s_xz)
    await_bytes(partr, s_grp)
    await_bytes(yr.at[:, rest_q], s_ret)
    await_bytes(rr.at[:, rest_y], s_rs)
    await_bytes(tr, s_tp)


def on_device(nz, nx, ny, master, gate_up, owner_map, tokens, routes, gate_weights):
    steps, rows, width = tokens.shape
    depth, experts, hid = master.shape
    top = routes.shape[2]
    nq = nz * nx
    slots = 2 * ny
    line = ny * rows
    vmem = pltpu.VMEM
    dma = pltpu.SemaphoreType.DMA
    scratch = [
        vmem((steps, rows, experts), f32),
        vmem((ny, steps, rows, experts), f32),
        vmem((steps, ny, rows, width), bf16),
        vmem((steps, nq, slots, width), bf16),
        vmem((steps, nq, slots, width), bf16),
        vmem((steps, 2, line, nq * slots), bf16),
        vmem((steps, 2, nq * slots, hid), f32),
        vmem((steps, 2, nq * slots, hid), f32),
        vmem((steps, nq, slots, width), bf16),
        vmem((steps, nq, slots, width), bf16),
        vmem((steps, ny, rows, width), bf16),
        vmem((steps, ny, rows, width), bf16),
        vmem((steps, rows, width), bf16),
        vmem((steps, rows, width), bf16),
        vmem((8, experts), f32),
        vmem((ny, 8, experts), f32),
        vmem((8, experts), f32),
        vmem((8, experts), f32),
        vmem((ny, 2, nq, depth // 2 * hid), bf16),
        vmem((ny, 2, nq, depth // 2 * hid), bf16),
        vmem((nq, 2 * ny, depth // 2 * hid), bf16),
        vmem((nq, 2 * ny, depth // 2 * hid), bf16),
        vmem((width, hid), bf16),
        vmem((width, width), bf16),
    ]
    scratch += [dma] * 11
    scratch += [
        dma((steps,)), dma, dma((steps,)), dma((steps,)), dma((steps,)), dma((steps,)), dma((steps,)),
        dma, dma, dma, dma,
    ]
    return pl.pallas_call(
        functools.partial(kernel, nz, nx, ny),
        out_shape=jax.ShapeDtypeStruct((steps, rows, width), bf16),
        in_specs=[pl.BlockSpec(memory_space=vmem)] * 6,
        out_specs=pl.BlockSpec(memory_space=vmem),
        scratch_shapes=scratch,
        compiler_params=pltpu.CompilerParams(
            collective_id=0, has_side_effects=True, vmem_limit_bytes=56 * 2**20
        ),
    )(
        master,
        gate_up[0],
        owner_map.reshape(1, experts),
        tokens,
        routes.reshape(steps * rows, top),
        gate_weights.reshape(steps * rows, top),
    )


def solution(mesh, sizes=(4, 4, 8)):
    placed = (
        P(("grp", "ep"), None, "tp"),
        P("ep", None, "grp", "tp"),
        P(),
        P(None, "ep", "grp"),
        P(None, "ep", None),
        P(None, "ep", None),
    )
    return jax.shard_map(
        functools.partial(on_device, *sizes),
        mesh=mesh, in_specs=placed, out_specs=P(None, "ep", "grp"), check_vma=False,
    )
```

```python
import functools

import jax
import jax.numpy as jnp
from jax import lax
from jax.experimental import pallas as pl
from jax.experimental.pallas import tpu as pltpu
from jax.sharding import PartitionSpec as P

f32 = jnp.float32
bf16 = jnp.bfloat16
NT = (((1,), (1,)), ((), ()))


def mm(a, b):
    return jnp.dot(a, b, preferred_element_type=f32)


def mm_nt(a, b):
    return lax.dot_general(a, b, NT, preferred_element_type=f32)


def iota(shape, dim):
    return lax.broadcasted_iota(jnp.int32, shape, dim)


def snap(values):
    magnitude = jnp.abs(values)
    magnitude = magnitude + magnitude * 2.0 ** (-22)
    large = magnitude * (2.0**20 + 1.0)
    fine = large - (large - magnitude)
    coarse = (magnitude + 24576.0) - 24576.0
    snapped = jnp.where(magnitude < 2.0 ** (-5), coarse, fine)
    return jnp.where(values < 0, -snapped, snapped)


def kernel(
    nz, nx, ny,
    master, gate_up, owner_map, tokens, routes, gates,
    out,
    wt, agw, ag, xs, x1, xr, cmb, part, partr, hd, ys, z1, yr, rs, rr, ts, tr,
    pk, pkr, pk2, pk2r, sa, c1, c2, sb, rb, wd,
    s_ag, s_agw, s_x, s_z, s_grp, s_rz, s_rx, s_rs, s_tp, s_pk, s_pk2, s_cx, s_cz, s_cy,
    r_ag, r_agw, r_x, r_z, r_grp, r_rz, r_rx, r_rs, r_tp, r_pk, r_pk2, r_cx, r_cz, r_cy,
):
    steps, rows, width = tokens.shape
    experts = owner_map.shape[1]
    top = routes.shape[1]
    depth, _, hid = master.shape
    parts = depth // 2
    nq = nz * nx
    slots = 2 * ny
    line = ny * rows
    g = lax.axis_index("grp")
    ep = lax.axis_index("ep")
    t = lax.axis_index("tp")
    z, x, y = ep // (nx * ny), (ep // ny) % nx, ep % ny
    zz = t * nz + z

    def y_peer(dy):
        return {"ep": ep - y + (y + dy + ny) % ny}

    def x_peer(dx):
        return {"ep": ep + ((x + dx + nx) % nx - x) * ny}

    def ring_peer(dz, sign):
        if 2 * dz < nz:
            off = dz
        elif 2 * dz > nz:
            off = dz - nz
        else:
            off = dz * (1 - 2 * g)
        zt = (zz + sign * off + 2 * nz) % (2 * nz)
        return {"ep": ep + (zt % nz - z) * (nx * ny), "tp": zt // nz}

    def group_peer(dz):
        return {"ep": ep + ((z + dz) % nz - z) * (nx * ny)}

    x_mate = {"ep": ep + (1 - 2 * (x % 2)) * ny}
    grp_mate = {"grp": 1 - g}
    tp_mate = {"tp": 1 - t}

    greeted = [y_peer(dy) for dy in range(1, ny)]
    greeted += [x_peer(dx) for dx in range(1, nx)]
    greeted += [ring_peer(dz, 1) for dz in range(1, nz)]
    greeted += [ring_peer(nz // 2, -1)]
    greeted += [group_peer(dz) for dz in range(1, nz)]
    greeted += [grp_mate, tp_mate]
    barrier = pltpu.get_barrier_semaphore()
    for peer in greeted:
        pl.semaphore_signal(barrier, inc=1, device_id=peer, device_id_type=pl.DeviceIdType.MESH)

    def send(src, dst, ssem, rsem, peer):
        pltpu.make_async_remote_copy(
            src_ref=src, dst_ref=dst, send_sem=ssem, recv_sem=rsem,
            device_id=peer, device_id_type=pl.DeviceIdType.MESH,
        ).start()

    def await_bytes(ref, sem):
        pltpu.make_async_copy(ref, ref, sem).wait()

    rest_x, rest_y, rest_z = pl.ds(1, nx - 1), pl.ds(1, ny - 1), pl.ds(1, nz - 1)

    cols = hid // 128
    lanes_p = iota((experts, 128), 1)
    peaks = jnp.zeros((experts, 128), f32)
    for j in range(cols):
        most = jnp.abs(master[0, :, j * 128:(j + 1) * 128])
        for d in range(1, depth):
            most = jnp.maximum(most, jnp.abs(master[d, :, j * 128:(j + 1) * 128]))
        peaks = jnp.where(lanes_p == j, jnp.max(most, axis=1, keepdims=True), peaks)
    pk[...] = peaks.T[:8]
    pkr[0] = pk[...]

    count = steps * rows
    blank = [jnp.zeros((top, experts - count), f32)]
    names = jnp.concatenate([routes[s].astype(f32) for s in range(steps)] + blank, axis=1)
    shares = jnp.concatenate([gates[s] for s in range(steps)] + blank, axis=1)
    index_e = iota((experts, experts), 0).astype(f32)
    weight_of = jnp.zeros((experts, experts), f32)
    for k in range(top):
        weight_of += jnp.where(names[k:k + 1, :] == index_e, shares[k:k + 1, :], 0.0)
    weight_of = weight_of.T[:count].reshape(steps, rows, experts)
    wt[...] = weight_of
    agw[0] = weight_of
    pl.semaphore_wait(barrier, len(greeted))

    for dy in range(1, ny):
        send(pk, pkr.at[dy], s_pk, r_pk, y_peer(dy))

    def gather_start(s, carry):
        for dy in range(1, ny):
            send(tokens.at[s], ag.at[s, dy], s_ag, r_ag.at[s], y_peer(dy))
        ag[s, 0] = tokens[s]
        return carry

    gather_start(0, 0)
    for dy in range(1, ny):
        send(wt, agw.at[dy], s_agw, r_agw, y_peer(dy))

    await_bytes(pkr.at[rest_y], r_pk)
    pk2[...] = jnp.max(pkr[...], axis=0)
    send(pk2, pk2r, s_pk2, r_pk2, x_mate)
    lax.fori_loop(1, steps, gather_start, 0)

    row_q = iota((nq * slots, 1), 0)
    peer_q = row_q // slots
    owner_q = (
        ((z + peer_q % nz) % nz) * (nx * ny) + ((x + peer_q // nz) % nx) * ny + y
    )
    pick = (owner_map[...] == owner_q).astype(f32).astype(bf16)
    slot_col = row_q % slots
    slot_row = iota((1, nq * slots), 1) % slots
    row_col = iota((line, 1), 0) // rows
    row_row = iota((1, line), 1) // rows
    la, lb = iota((line, line), 0), iota((line, line), 1)
    lower = ((la // rows == lb // rows) & (lb < la)).astype(f32).astype(bf16)
    spot = ((slot_col // 2) == row_row)
    spot_t = ((slot_row // 2) == row_col)
    order_col = (slot_col % 2 + 1).astype(f32)
    order_row = (slot_row % 2 + 1).astype(f32)

    twice = 2 * experts
    row_p = iota((twice, 1), 0)
    owner_p = (
        ((z + (row_p // slots) % nz) % nz) * (nx * ny)
        + ((x + row_p // (slots * nz)) % nx) * ny
        + (y + (row_p // 2) % ny) % ny
    )
    owner_two = jnp.concatenate([owner_map[...], owner_map[...]], axis=1)
    half_two = iota((1, twice), 1) // experts
    order_p = ((owner_two == owner_p) & (half_two == row_p % 2)).astype(f32).astype(bf16)

    await_bytes(pk2r, r_pk2)
    both = jnp.maximum(pk2[...], pk2r[...])
    scale_t = (both + 1e-06) / 448.0
    scale = jnp.concatenate([scale_t, jnp.ones((128 - 8, experts), f32)], axis=0).T
    inverse = 1.0 / scale

    def code(c, carry):
        halves = []
        for h in range(2):
            pieces = []
            for j in range(cols):
                field = master[h * parts + c, :, j * 128:(j + 1) * 128]
                pieces.append((snap(field * inverse[:, j:j + 1]) * scale[:, j:j + 1]).astype(bf16))
            halves.append(jnp.concatenate(pieces, axis=1))
        moved = mm(order_p, jnp.concatenate(halves, axis=0))
        moved = moved.astype(bf16).reshape(nx, nz, slots, hid)
        sa[c] = moved
        for dx in range(1, nx):
            send(sa.at[c, dx], c1.at[c, dx], s_cx, r_cx.at[c], x_peer(dx))
        c1[c, 0] = sa[c, 0]
        return carry

    lax.fori_loop(0, parts, code, 0)

    def code_z(c):
        await_bytes(c1.at[c, rest_x], r_cx.at[c])
        for dz in range(1, nz):
            send(c1.at[c, :, dz], c2.at[c, dz], s_cz, r_cz.at[c], group_peer(dz))
        c2[c, 0] = c1[c, :, 0]

    ra_, rb_ = iota((twice, 1), 0), iota((1, twice), 1)
    per_y = 2 * nq
    regroup = (
        rb_ == ((ra_ % per_y) // 2) * slots + (ra_ // per_y) * 2 + ra_ % 2
    ).astype(f32).astype(bf16)

    def code_y(c):
        await_bytes(c2.at[c, rest_z], r_cz.at[c])
        moved = mm(regroup, c2[c].reshape(twice, hid)).astype(bf16).reshape(ny, per_y, hid)
        sb[c] = moved
        for dy in range(1, ny):
            send(sb.at[c, dy], rb.at[c, dy], s_cy, r_cy.at[c], y_peer(dy))
        rb[c, 0] = sb[c, 0]

    row_r = iota((twice, 1), 0)
    source_r = (
        ((z - row_r // (2 * nx) % nz + nz) % nz) * (nx * ny)
        + ((x - (row_r // 2) % nx + nx) % nx) * ny
        + (y - row_r // per_y + ny) % ny
    )
    base_r = source_r * depth + (row_r % 2) * parts
    feature = iota((1, width), 1)

    def place(c):
        await_bytes(rb.at[c, rest_y], r_cy.at[c])
        spread = (feature == base_r + c).astype(f32).astype(bf16)
        piece = lax.dot_general(
            rb[c].reshape(twice, hid), spread, (((0,), (0,)), ((), ())), preferred_element_type=f32
        ).astype(bf16)

        @pl.when(c == 0)
        def _():
            wd[...] = piece

        @pl.when(c > 0)
        def _():
            wd[...] = wd[...] + piece

    def dispatch(s):
        weights = agw[:, s].reshape(line, experts)
        named = (weights > 0).astype(f32)
        ahead = mm(lower, named.astype(bf16))
        turn = (named * (ahead + 1.0)).astype(bf16)
        chosen = (mm_nt(pick, turn) == order_col) & spot
        await_bytes(ag.at[s, rest_y], r_ag.at[s])
        moved = mm(chosen.astype(f32).astype(bf16), ag[s].reshape(line, width))
        xs[s] = moved.astype(bf16).reshape(nx, nz, slots, width)
        for dx in range(1, nx):
            send(xs.at[s, dx], x1.at[s, dx], s_x, r_x.at[s], x_peer(dx))
        x1[s, 0] = xs[s, 0]
        kept = (mm_nt(turn, pick) == order_row) & spot_t
        upper = weights.astype(bf16)
        lesser = (weights - upper.astype(f32)).astype(bf16)
        cmb[s, 0] = jnp.where(kept, mm_nt(upper, pick), 0.0).astype(bf16)
        cmb[s, 1] = jnp.where(kept, mm_nt(lesser, pick), 0.0).astype(bf16)

    def relay(s):
        await_bytes(x1.at[s, rest_x], r_x.at[s])
        for dz in range(1, nz):
            send(x1.at[s, :, dz], xr.at[s, dz], s_z, r_z.at[s], ring_peer(dz, 1))
        xr[s, 0] = x1[s, :, 0]

    def expert_in(s):
        await_bytes(xr.at[s, rest_z], r_z.at[s])
        items = xr[s].reshape(nq * slots, width)
        part[s, 0] = mm(items, gate_up[0])
        part[s, 1] = mm(items, gate_up[1])
        send(part.at[s], partr.at[s], s_grp, r_grp.at[s], grp_mate)

    def expert_mid(s):
        await_bytes(partr.at[s], r_grp.at[s])
        gated = part[s, 0] + partr[s, 0]
        upped = part[s, 1] + partr[s, 1]
        hd[s] = (gated / (1.0 + jnp.exp(-gated)) * upped).astype(bf16)

    def expert_out(s, carry):
        result = mm(hd[s], wd[...])
        ys[s] = result.astype(bf16).reshape(nz, nx, slots, width)
        for dz in range(1, nz):
            send(ys.at[s, dz], z1.at[s, dz], s_rz, r_rz.at[s], ring_peer(dz, -1))
        z1[s, 0] = ys[s, 0]
        return carry

    def relay_back(s):
        await_bytes(z1.at[s, rest_z], r_rz.at[s])
        for dx in range(1, nx):
            send(z1.at[s, :, dx], yr.at[s, dx], s_rx, r_rx.at[s], x_peer(-dx))
        yr[s, 0] = z1[s, :, 0]

    def combine(s):
        await_bytes(yr.at[s, rest_x], r_rx.at[s])
        items = yr[s].reshape(nq * slots, width)
        mixed = mm(cmb[s, 0], items) + mm(cmb[s, 1], items)
        rs[s] = mixed.astype(bf16).reshape(ny, rows, width)
        for dy in range(1, ny):
            send(rs.at[s, dy], rr.at[s, dy], s_rs, r_rs.at[s], y_peer(-dy))
        rr[s, 0] = rs[s, 0]

    def total(s):
        await_bytes(rr.at[s, rest_y], r_rs.at[s])
        mixed = rr[s, 0].astype(f32)
        for dy in range(1, ny):
            mixed += rr[s, dy].astype(f32)
        ts[s] = mixed.astype(bf16)
        send(ts.at[s], tr.at[s], s_tp, r_tp.at[s], tp_mate)

    def finish(s):
        await_bytes(tr.at[s], r_tp.at[s])
        out[s] = (ts[s].astype(f32) + tr[s].astype(f32)).astype(bf16)

    def staged(i, plan, upto):
        for stage, lag in plan:
            @pl.when((i >= lag) & (i < lag + upto))
            def _():
                stage(i - lag)

    await_bytes(agw.at[rest_y], r_agw)

    def forth(i, carry):
        staged(i, [(dispatch, 0), (code_z, 0), (relay, 1), (code_y, 1), (expert_in, 2), (place, 2), (expert_mid, 2)], steps)
        return carry

    def back(i, carry):
        staged(i, [(relay_back, 0), (combine, 1), (total, 2), (finish, 3)], steps)
        return carry

    lax.fori_loop(0, steps + 2, forth, 0)
    lax.fori_loop(0, steps, expert_out, 0)
    lax.fori_loop(0, steps + 3, back, 0)

    await_bytes(agw.at[rest_y], s_agw)
    await_bytes(ag.at[:, rest_y], s_ag)
    await_bytes(pkr.at[rest_y], s_pk)
    await_bytes(pk2r, s_pk2)
    await_bytes(c1.at[:, rest_x], s_cx)
    await_bytes(c2.at[:, rest_z], s_cz)
    await_bytes(rb.at[:, rest_y], s_cy)
    await_bytes(x1.at[:, rest_x], s_x)
    await_bytes(xr.at[:, rest_z], s_z)
    await_bytes(partr, s_grp)
    await_bytes(z1.at[:, rest_z], s_rz)
    await_bytes(yr.at[:, rest_x], s_rx)
    await_bytes(rr.at[:, rest_y], s_rs)
    await_bytes(tr, s_tp)


def on_device(nz, nx, ny, master, gate_up, owner_map, tokens, routes, gate_weights):
    steps, rows, width = tokens.shape
    depth, experts, hid = master.shape
    parts = depth // 2
    nq = nz * nx
    slots = 2 * ny
    line = ny * rows
    vmem = pltpu.VMEM
    dma = pltpu.SemaphoreType.DMA
    by_x = vmem((steps, nx, nz, slots, width), bf16)
    by_z = vmem((steps, nz, nx, slots, width), bf16)
    by_y = vmem((steps, ny, rows, width), bf16)
    sums = vmem((steps, 2, nq * slots, hid), f32)
    own = vmem((steps, rows, width), bf16)
    peak = vmem((8, experts), f32)
    code_x = vmem((parts, nx, nz, slots, hid), bf16)
    code_z = vmem((parts, nz, nx, slots, hid), bf16)
    code_y = vmem((parts, ny, 2 * nq, hid), bf16)
    scratch = [
        vmem((steps, rows, experts), f32),
        vmem((ny, steps, rows, experts), f32),
        by_y, by_x, by_x, by_z,
        vmem((steps, 2, line, nq * slots), bf16),
        sums, sums,
        vmem((steps, nq * slots, hid), bf16),
        by_z, by_z, by_x, by_y, by_y, own, own,
        peak, vmem((ny, 8, experts), f32), peak, peak,
        code_x, code_x, code_z, code_y, code_y,
        vmem((hid, width), bf16),
    ]
    per_step, per_part = dma((steps,)), dma((parts,))
    scratch += [dma] * 14
    scratch += [
        per_step, dma, per_step, per_step, per_step, per_step, per_step, per_step, per_step,
        dma, dma, per_part, per_part, per_part,
    ]
    return pl.pallas_call(
        functools.partial(kernel, nz, nx, ny),
        out_shape=jax.ShapeDtypeStruct((steps, rows, width), bf16),
        in_specs=[pl.BlockSpec(memory_space=vmem)] * 6,
        out_specs=pl.BlockSpec(memory_space=vmem),
        scratch_shapes=scratch,
        compiler_params=pltpu.CompilerParams(
            collective_id=0, has_side_effects=True, vmem_limit_bytes=56 * 2**20
        ),
    )(
        master,
        gate_up[0],
        owner_map.reshape(1, experts),
        tokens,
        jnp.swapaxes(routes, 1, 2),
        jnp.swapaxes(gate_weights, 1, 2),
    )


def solution(mesh, sizes=(4, 4, 8)):
    placed = (
        P(("grp", "ep"), None, "tp"),
        P("ep", None, "grp", "tp"),
        P(),
        P(None, "ep", "grp"),
        P(None, "ep", None),
        P(None, "ep", None),
    )
    return jax.shard_map(
        functools.partial(on_device, *sizes),
        mesh=mesh, in_specs=placed, out_specs=P(None, "ep", "grp"), check_vma=False,
    )
```

```python
import functools

import jax
import jax.numpy as jnp
from jax import lax
from jax.experimental import pallas as pl
from jax.experimental.pallas import tpu as pltpu
from jax.sharding import PartitionSpec as P

f32 = jnp.float32
bf16 = jnp.bfloat16
NT = (((1,), (1,)), ((), ()))


def mm(a, b):
    return jnp.dot(a, b, preferred_element_type=f32)


def mm_nt(a, b):
    return lax.dot_general(a, b, NT, preferred_element_type=f32)


def iota(shape, dim):
    return lax.broadcasted_iota(jnp.int32, shape, dim)


def snap(values):
    magnitude = jnp.abs(values)
    magnitude = magnitude + magnitude * 2.0 ** (-22)
    large = magnitude * (2.0**20 + 1.0)
    fine = large - (large - magnitude)
    coarse = (magnitude + 24576.0) - 24576.0
    snapped = jnp.where(magnitude < 2.0 ** (-5), coarse, fine)
    return jnp.where(values < 0, -snapped, snapped)


def kernel(
    nz, nx, ny,
    master, gate_up, owner_map, tokens, routes, gates,
    out,
    nm, nmr, agw, ag, xs, x1, xr, cmb, part, partr, hd, ys, z1, yr, rs, rr, ts, tr,
    pk, pkr, pk2, pk2r, sa, c1, c2, sb, rb, wd,
    s_ag, s_nm, s_x, s_z, s_grp, s_rz, s_rx, s_rs, s_tp, s_pk, s_pk2, s_cx, s_cz, s_cy,
    r_ag, r_nm, r_x, r_z, r_grp, r_rz, r_rx, r_rs, r_tp, r_pk, r_pk2, r_cx, r_cz, r_cy,
):
    steps, rows, width = tokens.shape
    experts = owner_map.shape[1]
    top = routes.shape[1]
    depth, _, hid = master.shape
    parts = depth // 2
    nq = nz * nx
    slots = 2 * ny
    line = ny * rows
    g = lax.axis_index("grp")
    ep = lax.axis_index("ep")
    t = lax.axis_index("tp")
    z, x, y = ep // (nx * ny), (ep // ny) % nx, ep % ny
    zz = t * nz + z

    def y_peer(dy):
        return {"ep": ep - y + (y + dy + ny) % ny}

    def x_peer(dx):
        return {"ep": ep + ((x + dx + nx) % nx - x) * ny}

    def ring_peer(dz, sign):
        if 2 * dz < nz:
            off = dz
        elif 2 * dz > nz:
            off = dz - nz
        else:
            off = dz * (1 - 2 * g)
        zt = (zz + sign * off + 2 * nz) % (2 * nz)
        return {"ep": ep + (zt % nz - z) * (nx * ny), "tp": zt // nz}

    def group_peer(dz):
        return {"ep": ep + ((z + dz) % nz - z) * (nx * ny)}

    x_mate = {"ep": ep + (1 - 2 * (x % 2)) * ny}
    grp_mate = {"grp": 1 - g}
    tp_mate = {"tp": 1 - t}

    greeted = [y_peer(dy) for dy in range(1, ny)]
    greeted += [x_peer(dx) for dx in range(1, nx)]
    greeted += [ring_peer(dz, 1) for dz in range(1, nz)]
    greeted += [ring_peer(nz // 2, -1)]
    greeted += [group_peer(dz) for dz in range(1, nz)]
    greeted += [grp_mate, tp_mate]
    barrier = pltpu.get_barrier_semaphore()
    for peer in greeted:
        pl.semaphore_signal(barrier, inc=1, device_id=peer, device_id_type=pl.DeviceIdType.MESH)

    def send(src, dst, ssem, rsem, peer):
        pltpu.make_async_remote_copy(
            src_ref=src, dst_ref=dst, send_sem=ssem, recv_sem=rsem,
            device_id=peer, device_id_type=pl.DeviceIdType.MESH,
        ).start()

    def await_bytes(ref, sem):
        pltpu.make_async_copy(ref, ref, sem).wait()

    rest_x, rest_y, rest_z = pl.ds(1, nx - 1), pl.ds(1, ny - 1), pl.ds(1, nz - 1)

    cols = hid // 128
    lanes_p = iota((experts, 128), 1)
    peaks = jnp.zeros((experts, 128), f32)
    for j in range(cols):
        most = jnp.abs(master[0, :, j * 128:(j + 1) * 128])
        for d in range(1, depth):
            most = jnp.maximum(most, jnp.abs(master[d, :, j * 128:(j + 1) * 128]))
        peaks = jnp.where(lanes_p == j, jnp.max(most, axis=1, keepdims=True), peaks)
    pk[...] = peaks.T[:8]
    pkr[0] = pk[...]
    ag[:, 0] = tokens[...]

    count = steps * rows
    blank = [jnp.zeros((top, experts - count), f32)]
    nm[0] = jnp.concatenate([routes[s].astype(f32) for s in range(steps)] + blank, axis=1)
    nm[1] = jnp.concatenate([gates[s] for s in range(steps)] + blank, axis=1)
    nmr[0] = nm[...]
    pl.semaphore_wait(barrier, len(greeted))

    for dy in range(1, ny):
        send(pk, pkr.at[dy], s_pk, r_pk, y_peer(dy))
    for dy in range(1, ny):
        send(nm, nmr.at[dy], s_nm, r_nm, y_peer(dy))

    def hop(s, h, sign):
        held = (h - 1) * sign % ny
        if h > 1:
            await_bytes(ag.at[s, held], r_ag.at[s, held])
        place_at = h * sign % ny
        send(ag.at[s, held], ag.at[s, place_at], s_ag, r_ag.at[s, place_at], y_peer(sign))

    def ring(h):
        if 2 * h < ny:
            def both_ways(s, carry):
                hop(s, h, 1)
                hop(s, h, -1)
                return carry

            lax.fori_loop(0, steps, both_ways, 0)
        else:
            for s in range(steps):
                hop(s, h, 1 - 2 * (s % 2))

    def ring_end(s):
        await_bytes(ag.at[s, ny // 2], r_ag.at[s, ny // 2])
        last = ny // 2 + 1 - 2 * (s % 2)
        await_bytes(ag.at[s, last], r_ag.at[s, last])

    ring(1)
    await_bytes(pkr.at[rest_y], r_pk)
    pk2[...] = jnp.max(pkr[...], axis=0)
    send(pk2, pk2r, s_pk2, r_pk2, x_mate)
    ring(2)

    row_q = iota((nq * slots, 1), 0)
    peer_q = row_q // slots
    owner_q = (
        ((z + peer_q % nz) % nz) * (nx * ny) + ((x + peer_q // nz) % nx) * ny + y
    )
    pick = (owner_map[...] == owner_q).astype(f32).astype(bf16)
    slot_col = row_q % slots
    slot_row = iota((1, nq * slots), 1) % slots
    row_col = iota((line, 1), 0) // rows
    row_row = iota((1, line), 1) // rows
    la, lb = iota((line, line), 0), iota((line, line), 1)
    lower = ((la // rows == lb // rows) & (lb < la)).astype(f32).astype(bf16)
    spot = ((slot_col // 2) == row_row)
    spot_t = ((slot_row // 2) == row_col)
    order_col = (slot_col % 2 + 1).astype(f32)
    order_row = (slot_row % 2 + 1).astype(f32)

    twice = 2 * experts
    row_p = iota((twice, 1), 0)
    owner_p = (
        ((z + (row_p // slots) % nz) % nz) * (nx * ny)
        + ((x + row_p // (slots * nz)) % nx) * ny
        + (y + (row_p // 2) % ny) % ny
    )
    owner_two = jnp.concatenate([owner_map[...], owner_map[...]], axis=1)
    half_two = iota((1, twice), 1) // experts
    order_p = ((owner_two == owner_p) & (half_two == row_p % 2)).astype(f32).astype(bf16)

    await_bytes(pk2r, r_pk2)
    both = jnp.maximum(pk2[...], pk2r[...])
    scale_t = (both + 1e-06) / 448.0
    scale = jnp.concatenate([scale_t, jnp.ones((128 - 8, experts), f32)], axis=0).T
    inverse = 1.0 / scale

    def code(c, carry):
        halves = []
        for h in range(2):
            pieces = []
            for j in range(cols):
                field = master[h * parts + c, :, j * 128:(j + 1) * 128]
                pieces.append((snap(field * inverse[:, j:j + 1]) * scale[:, j:j + 1]).astype(bf16))
            halves.append(jnp.concatenate(pieces, axis=1))
        moved = mm(order_p, jnp.concatenate(halves, axis=0))
        moved = moved.astype(bf16).reshape(nx, nz, slots, hid)
        sa[c] = moved
        for dx in range(1, nx):
            send(sa.at[c, dx], c1.at[c, dx], s_cx, r_cx.at[c], x_peer(dx))
        c1[c, 0] = sa[c, 0]
        return carry

    def code_z(c):
        await_bytes(c1.at[c, rest_x], r_cx.at[c])
        for dz in range(1, nz):
            send(c1.at[c, :, dz], c2.at[c, dz], s_cz, r_cz.at[c], group_peer(dz))
        c2[c, 0] = c1[c, :, 0]

    code(0, 0)
    ring(3)
    code(1, 0)
    code_z(0)
    for h in range(4, ny // 2 + 1):
        ring(h)
    code(2, 0)
    code_z(1)
    code(3, 0)

    ra_, rb_ = iota((twice, 1), 0), iota((1, twice), 1)
    per_y = 2 * nq
    regroup = (
        rb_ == ((ra_ % per_y) // 2) * slots + (ra_ // per_y) * 2 + ra_ % 2
    ).astype(f32).astype(bf16)

    def code_y(c):
        await_bytes(c2.at[c, rest_z], r_cz.at[c])
        moved = mm(regroup, c2[c].reshape(twice, hid)).astype(bf16).reshape(ny, per_y, hid)
        sb[c] = moved
        for dy in range(1, ny):
            send(sb.at[c, dy], rb.at[c, dy], s_cy, r_cy.at[c], y_peer(dy))
        rb[c, 0] = sb[c, 0]

    row_r = iota((twice, 1), 0)
    source_r = (
        ((z - row_r // (2 * nx) % nz + nz) % nz) * (nx * ny)
        + ((x - (row_r // 2) % nx + nx) % nx) * ny
        + (y - row_r // per_y + ny) % ny
    )
    base_r = source_r * depth + (row_r % 2) * parts
    feature = iota((1, width), 1)

    def place(c):
        await_bytes(rb.at[c, rest_y], r_cy.at[c])
        spread = (feature == base_r + c).astype(f32).astype(bf16)
        piece = lax.dot_general(
            rb[c].reshape(twice, hid), spread, (((0,), (0,)), ((), ())), preferred_element_type=f32
        ).astype(bf16)

        @pl.when(c == 0)
        def _():
            wd[...] = piece

        @pl.when(c > 0)
        def _():
            wd[...] = wd[...] + piece

    def dispatch(s):
        weights = agw[:, s].reshape(line, experts)
        named = (weights > 0).astype(f32)
        ahead = mm(lower, named.astype(bf16))
        turn = (named * (ahead + 1.0)).astype(bf16)
        chosen = (mm_nt(pick, turn) == order_col) & spot
        ring_end(s)
        moved = mm(chosen.astype(f32).astype(bf16), ag[s].reshape(line, width))
        xs[s] = moved.astype(bf16).reshape(nx, nz, slots, width)
        for dx in range(1, nx):
            send(xs.at[s, dx], x1.at[s, dx], s_x, r_x.at[s], x_peer(dx))
        x1[s, 0] = xs[s, 0]
        kept = (mm_nt(turn, pick) == order_row) & spot_t
        upper = weights.astype(bf16)
        lesser = (weights - upper.astype(f32)).astype(bf16)
        cmb[s, 0] = jnp.where(kept, mm_nt(upper, pick), 0.0).astype(bf16)
        cmb[s, 1] = jnp.where(kept, mm_nt(lesser, pick), 0.0).astype(bf16)

    def relay(s):
        await_bytes(x1.at[s, rest_x], r_x.at[s])
        for dz in range(1, nz):
            send(x1.at[s, :, dz], xr.at[s, dz], s_z, r_z.at[s], ring_peer(dz, 1))
        xr[s, 0] = x1[s, :, 0]

    def expert_in(s):
        await_bytes(xr.at[s, rest_z], r_z.at[s])
        items = xr[s].reshape(nq * slots, width)
        part[s, 0] = mm(items, gate_up[0])
        part[s, 1] = mm(items, gate_up[1])
        send(part.at[s], partr.at[s], s_grp, r_grp.at[s], grp_mate)

    def expert_mid(s):
        await_bytes(partr.at[s], r_grp.at[s])
        gated = part[s, 0] + partr[s, 0]
        upped = part[s, 1] + partr[s, 1]
        hd[s] = (gated / (1.0 + jnp.exp(-gated)) * upped).astype(bf16)

    def expert_out(s, carry):
        result = mm(hd[s], wd[...])
        ys[s] = result.astype(bf16).reshape(nz, nx, slots, width)
        for dz in range(1, nz):
            send(ys.at[s, dz], z1.at[s, dz], s_rz, r_rz.at[s], ring_peer(dz, -1))
        z1[s, 0] = ys[s, 0]
        return carry

    def relay_back(s):
        await_bytes(z1.at[s, rest_z], r_rz.at[s])
        for dx in range(1, nx):
            send(z1.at[s, :, dx], yr.at[s, dx], s_rx, r_rx.at[s], x_peer(-dx))
        yr[s, 0] = z1[s, :, 0]

    def combine(s):
        await_bytes(yr.at[s, rest_x], r_rx.at[s])
        items = yr[s].reshape(nq * slots, width)
        mixed = mm(cmb[s, 0], items) + mm(cmb[s, 1], items)
        rs[s] = mixed.astype(bf16).reshape(ny, rows, width)
        for dy in range(1, ny):
            send(rs.at[s, dy], rr.at[s, dy], s_rs, r_rs.at[s], y_peer(-dy))
        rr[s, 0] = rs[s, 0]

    def total(s):
        await_bytes(rr.at[s, rest_y], r_rs.at[s])
        mixed = rr[s, 0].astype(f32)
        for dy in range(1, ny):
            mixed += rr[s, dy].astype(f32)
        ts[s] = mixed.astype(bf16)
        send(ts.at[s], tr.at[s], s_tp, r_tp.at[s], tp_mate)

    def finish(s):
        await_bytes(tr.at[s], r_tp.at[s])
        out[s] = (ts[s].astype(f32) + tr[s].astype(f32)).astype(bf16)

    def staged(i, plan, upto):
        for stage, lag in plan:
            @pl.when((i >= lag) & (i < lag + upto))
            def _():
                stage(i - lag)

    await_bytes(nmr.at[rest_y], r_nm)
    index_e = iota((experts, experts), 0).astype(f32)

    def spread_weights(dy, carry):
        names, shares = nmr[dy, 0], nmr[dy, 1]
        weight_of = jnp.zeros((experts, experts), f32)
        for k in range(top):
            weight_of += jnp.where(names[k:k + 1, :] == index_e, shares[k:k + 1, :], 0.0)
        agw[dy] = weight_of.T[:count].reshape(steps, rows, experts)
        return carry

    lax.fori_loop(0, ny, spread_weights, 0)

    def forth(i, carry):
        staged(i, [(dispatch, 0), (code_z, -2), (code_y, 0), (relay, 1), (place, 1), (expert_mid, 3)], steps)
        first = jnp.where(i < steps + 1, 0, i - steps + 1)
        lax.fori_loop(first, jnp.where(i < steps, 0, i - steps + 2), expert_out, 0)
        staged(i, [(expert_in, 2)], steps)
        return carry

    def back(i, carry):
        staged(i, [(relay_back, 0), (combine, 1), (total, 2), (finish, 3)], steps)
        return carry

    lax.fori_loop(0, steps + 3, forth, 0)
    lax.fori_loop(0, steps + 3, back, 0)

    await_bytes(nmr.at[rest_y], s_nm)
    await_bytes(ag.at[:, rest_y], s_ag)
    await_bytes(pkr.at[rest_y], s_pk)
    await_bytes(pk2r, s_pk2)
    await_bytes(c1.at[:, rest_x], s_cx)
    await_bytes(c2.at[:, rest_z], s_cz)
    await_bytes(rb.at[:, rest_y], s_cy)
    await_bytes(x1.at[:, rest_x], s_x)
    await_bytes(xr.at[:, rest_z], s_z)
    await_bytes(partr, s_grp)
    await_bytes(z1.at[:, rest_z], s_rz)
    await_bytes(yr.at[:, rest_x], s_rx)
    await_bytes(rr.at[:, rest_y], s_rs)
    await_bytes(tr, s_tp)


def on_device(nz, nx, ny, master, gate_up, owner_map, tokens, routes, gate_weights):
    steps, rows, width = tokens.shape
    depth, experts, hid = master.shape
    top_rows = routes.shape[2]
    parts = depth // 2
    nq = nz * nx
    slots = 2 * ny
    line = ny * rows
    vmem = pltpu.VMEM
    dma = pltpu.SemaphoreType.DMA
    by_x = vmem((steps, nx, nz, slots, width), bf16)
    by_z = vmem((steps, nz, nx, slots, width), bf16)
    by_y = vmem((steps, ny, rows, width), bf16)
    own = vmem((steps, rows, width), bf16)
    sums = vmem((steps, 2, nq * slots, hid), f32)
    named = vmem((2, top_rows, experts), f32)
    peak = vmem((8, experts), f32)
    code_x = vmem((parts, nx, nz, slots, hid), bf16)
    code_z = vmem((parts, nz, nx, slots, hid), bf16)
    code_y = vmem((parts, ny, 2 * nq, hid), bf16)
    scratch = [
        named, vmem((ny, 2, top_rows, experts), f32),
        vmem((ny, steps, rows, experts), f32),
        by_y, by_x, by_x, by_z,
        vmem((steps, 2, line, nq * slots), bf16),
        sums, sums,
        vmem((steps, nq * slots, hid), bf16),
        by_z, by_z, by_x, by_y, by_y, own, own,
        peak, vmem((ny, 8, experts), f32), peak, peak,
        code_x, code_x, code_z, code_y, code_y,
        vmem((hid, width), bf16),
    ]
    per_step, per_part = dma((steps,)), dma((parts,))
    scratch += [dma] * 14
    scratch += [
        dma((steps, ny)), dma, per_step, per_step, per_step, per_step, per_step, per_step, per_step,
        dma, dma, per_part, per_part, per_part,
    ]
    return pl.pallas_call(
        functools.partial(kernel, nz, nx, ny),
        out_shape=jax.ShapeDtypeStruct((steps, rows, width), bf16),
        in_specs=[pl.BlockSpec(memory_space=vmem)] * 6,
        out_specs=pl.BlockSpec(memory_space=vmem),
        scratch_shapes=scratch,
        compiler_params=pltpu.CompilerParams(
            collective_id=0, has_side_effects=True, vmem_limit_bytes=56 * 2**20
        ),
    )(
        master,
        gate_up[0],
        owner_map.reshape(1, experts),
        tokens,
        jnp.swapaxes(routes, 1, 2),
        jnp.swapaxes(gate_weights, 1, 2),
    )


def solution(mesh, sizes=(4, 4, 8)):
    placed = (
        P(("grp", "ep"), None, "tp"),
        P("ep", None, "grp", "tp"),
        P(),
        P(None, "ep", "grp"),
        P(None, "ep", None),
        P(None, "ep", None),
    )
    return jax.shard_map(
        functools.partial(on_device, *sizes),
        mesh=mesh, in_specs=placed, out_specs=P(None, "ep", "grp"), check_vma=False,
    )
```

```python
import functools

import jax
import jax.numpy as jnp
from jax import lax
from jax.experimental import pallas as pl
from jax.experimental.pallas import tpu as pltpu
from jax.sharding import PartitionSpec as P

f32 = jnp.float32
bf16 = jnp.bfloat16
NT = (((1,), (1,)), ((), ()))


def mm(a, b):
    return jnp.dot(a, b, preferred_element_type=f32)


def mm_nt(a, b):
    return lax.dot_general(a, b, NT, preferred_element_type=f32)


def iota(shape, dim):
    return lax.broadcasted_iota(jnp.int32, shape, dim)


def snap(values):
    magnitude = jnp.abs(values)
    magnitude = magnitude + magnitude * 2.0 ** (-22)
    large = magnitude * (2.0**20 + 1.0)
    fine = large - (large - magnitude)
    coarse = (magnitude + 24576.0) - 24576.0
    snapped = jnp.where(magnitude < 2.0 ** (-5), coarse, fine)
    return jnp.where(values < 0, -snapped, snapped)


def kernel(
    nz, nx, ny,
    master, gate_up, owner_map, tokens, routes, gates,
    out,
    nm, nmr, agw, ag, xs, x1, xr, cmb, part, partr, hd, ys, x2, yr, rs, rr, ts, tr,
    pk, pkr, pk2, pk2r, sa, c1, c2, sb, rb, wd,
    s_ag, s_nm, s_x, s_z, s_grp, s_rz, s_rx, s_rs, s_tp, s_pk, s_pk2, s_cx, s_cz, s_cy,
    r_ag, r_nm, r_x, r_z, r_grp, r_rz, r_rx, r_rs, r_tp, r_pk, r_pk2, r_cx, r_cz, r_cy,
):
    steps, rows, width = tokens.shape
    experts = owner_map.shape[1]
    top = routes.shape[1]
    depth, _, hid = master.shape
    parts = depth // 2
    nq = nz * nx
    slots = 2 * ny
    line = ny * rows
    wide = width // 2
    g = lax.axis_index("grp")
    ep = lax.axis_index("ep")
    t = lax.axis_index("tp")
    z, x, y = ep // (nx * ny), (ep // ny) % nx, ep % ny
    zz = t * nz + z

    def y_peer(dy):
        return {"ep": ep - y + (y + dy + ny) % ny}

    def x_peer(dx):
        return {"ep": ep + ((x + dx + nx) % nx - x) * ny}

    def ring_peer(dz, sign):
        if 2 * dz < nz:
            off = dz
        elif 2 * dz > nz:
            off = dz - nz
        else:
            off = dz * (1 - 2 * g)
        zt = (zz + sign * off + 2 * nz) % (2 * nz)
        return {"ep": ep + (zt % nz - z) * (nx * ny), "tp": zt // nz}

    def group_peer(dz):
        return {"ep": ep + ((z + dz) % nz - z) * (nx * ny)}

    x_mate = {"ep": ep + (1 - 2 * (x % 2)) * ny}
    grp_mate = {"grp": 1 - g}
    tp_mate = {"tp": 1 - t}

    greeted = [y_peer(dy) for dy in range(1, ny)]
    greeted += [x_peer(dx) for dx in range(1, nx)]
    greeted += [ring_peer(dz, 1) for dz in range(1, nz)]
    greeted += [ring_peer(nz // 2, -1)]
    greeted += [group_peer(dz) for dz in range(1, nz)]
    greeted += [grp_mate, tp_mate]
    barrier = pltpu.get_barrier_semaphore()
    for peer in greeted:
        pl.semaphore_signal(barrier, inc=1, device_id=peer, device_id_type=pl.DeviceIdType.MESH)

    def send(src, dst, ssem, rsem, peer):
        pltpu.make_async_remote_copy(
            src_ref=src, dst_ref=dst, send_sem=ssem, recv_sem=rsem,
            device_id=peer, device_id_type=pl.DeviceIdType.MESH,
        ).start()

    def await_bytes(ref, sem):
        pltpu.make_async_copy(ref, ref, sem).wait()

    rest_x, rest_y, rest_z = pl.ds(1, nx - 1), pl.ds(1, ny - 1), pl.ds(1, nz - 1)

    cols = hid // 128
    lanes_p = iota((experts, 128), 1)
    peaks = jnp.zeros((experts, 128), f32)
    for j in range(cols):
        most = jnp.abs(master[0, :, j * 128:(j + 1) * 128])
        for d in range(1, depth):
            most = jnp.maximum(most, jnp.abs(master[d, :, j * 128:(j + 1) * 128]))
        peaks = jnp.where(lanes_p == j, jnp.max(most, axis=1, keepdims=True), peaks)
    pk[...] = peaks.T[:8]
    pkr[0] = pk[...]
    ag[:, 0] = tokens[...]

    count = steps * rows
    blank = [jnp.zeros((top, experts - count), f32)]
    nm[0] = jnp.concatenate([routes[s].astype(f32) for s in range(steps)] + blank, axis=1)
    nm[1] = jnp.concatenate([gates[s] for s in range(steps)] + blank, axis=1)
    nmr[0] = nm[...]
    pl.semaphore_wait(barrier, len(greeted))

    for dy in range(1, ny):
        send(pk, pkr.at[dy], s_pk, r_pk, y_peer(dy))
    for dy in range(1, ny):
        send(nm, nmr.at[dy], s_nm, r_nm, y_peer(dy))

    def hop(s, h, sign):
        held = (h - 1) * sign % ny
        if h > 1:
            await_bytes(ag.at[s, held], r_ag.at[s, held])
        place_at = h * sign % ny
        send(ag.at[s, held], ag.at[s, place_at], s_ag, r_ag.at[s, place_at], y_peer(sign))

    def ring(h):
        if 2 * h < ny:
            def both_ways(s, carry):
                hop(s, h, 1)
                hop(s, h, -1)
                return carry

            lax.fori_loop(0, steps, both_ways, 0)
        else:
            for s in range(steps):
                hop(s, h, 1 - 2 * (s % 2))

    def ring_end(s):
        await_bytes(ag.at[s, ny // 2], r_ag.at[s, ny // 2])
        last = ny // 2 + 1 - 2 * (s % 2)
        await_bytes(ag.at[s, last], r_ag.at[s, last])

    ring(1)
    await_bytes(pkr.at[rest_y], r_pk)
    pk2[...] = jnp.max(pkr[...], axis=0)
    send(pk2, pk2r, s_pk2, r_pk2, x_mate)
    ring(2)

    row_q = iota((nq * slots, 1), 0)
    peer_q = row_q // slots
    owner_q = (
        ((z + peer_q % nz) % nz) * (nx * ny) + ((x + peer_q // nz) % nx) * ny + y
    )
    pick = (owner_map[...] == owner_q).astype(f32).astype(bf16)
    owner_b = (
        ((z + peer_q // nx) % nz) * (nx * ny) + ((x + peer_q % nx) % nx) * ny + y
    )
    pick_back = (owner_map[...] == owner_b).astype(f32).astype(bf16)
    slot_col = row_q % slots
    slot_row = iota((1, nq * slots), 1) % slots
    row_col = iota((line, 1), 0) // rows
    row_row = iota((1, line), 1) // rows
    la, lb = iota((line, line), 0), iota((line, line), 1)
    lower = ((la // rows == lb // rows) & (lb < la)).astype(f32).astype(bf16)
    spot = ((slot_col // 2) == row_row)
    spot_t = ((slot_row // 2) == row_col)
    order_col = (slot_col % 2 + 1).astype(f32)
    order_row = (slot_row % 2 + 1).astype(f32)

    twice = 2 * experts
    row_p = iota((twice, 1), 0)
    owner_p = (
        ((z + (row_p // slots) % nz) % nz) * (nx * ny)
        + ((x + row_p // (slots * nz)) % nx) * ny
        + (y + (row_p // 2) % ny) % ny
    )
    owner_two = jnp.concatenate([owner_map[...], owner_map[...]], axis=1)
    half_two = iota((1, twice), 1) // experts
    order_p = ((owner_two == owner_p) & (half_two == row_p % 2)).astype(f32).astype(bf16)

    await_bytes(pk2r, r_pk2)
    both = jnp.maximum(pk2[...], pk2r[...])
    scale_t = (both + 1e-06) / 448.0
    scale = jnp.concatenate([scale_t, jnp.ones((128 - 8, experts), f32)], axis=0).T
    inverse = 1.0 / scale

    def code(c, carry):
        halves = []
        for h in range(2):
            pieces = []
            for j in range(cols):
                field = master[h * parts + c, :, j * 128:(j + 1) * 128]
                pieces.append((snap(field * inverse[:, j:j + 1]) * scale[:, j:j + 1]).astype(bf16))
            halves.append(jnp.concatenate(pieces, axis=1))
        moved = mm(order_p, jnp.concatenate(halves, axis=0))
        moved = moved.astype(bf16).reshape(nx, nz, slots, hid)
        sa[c] = moved
        for dx in range(1, nx):
            send(sa.at[c, dx], c1.at[c, dx], s_cx, r_cx.at[c], x_peer(dx))
        c1[c, 0] = sa[c, 0]
        return carry

    def code_z(c):
        await_bytes(c1.at[c, rest_x], r_cx.at[c])
        for dz in range(1, nz):
            send(c1.at[c, :, dz], c2.at[c, dz], s_cz, r_cz.at[c], group_peer(dz))
        c2[c, 0] = c1[c, :, 0]

    code(0, 0)
    ring(3)
    code(1, 0)
    code_z(0)
    for h in range(4, ny // 2 + 1):
        ring(h)
    code(2, 0)
    code_z(1)
    code(3, 0)

    ra_, rb_ = iota((twice, 1), 0), iota((1, twice), 1)
    per_y = 2 * nq
    regroup = (
        rb_ == ((ra_ % per_y) // 2) * slots + (ra_ // per_y) * 2 + ra_ % 2
    ).astype(f32).astype(bf16)

    def code_y(c):
        await_bytes(c2.at[c, rest_z], r_cz.at[c])
        moved = mm(regroup, c2[c].reshape(twice, hid)).astype(bf16).reshape(ny, per_y, hid)
        sb[c] = moved
        for dy in range(1, ny):
            send(sb.at[c, dy], rb.at[c, dy], s_cy, r_cy.at[c], y_peer(dy))
        rb[c, 0] = sb[c, 0]

    row_r = iota((twice, 1), 0)
    source_r = (
        ((z - row_r // (2 * nx) % nz + nz) % nz) * (nx * ny)
        + ((x - (row_r // 2) % nx + nx) % nx) * ny
        + (y - row_r // per_y + ny) % ny
    )
    base_r = source_r * depth + (row_r % 2) * parts
    feature = iota((1, width), 1)

    def place(c):
        await_bytes(rb.at[c, rest_y], r_cy.at[c])
        spread = (feature == base_r + c).astype(f32).astype(bf16)
        piece = lax.dot_general(
            rb[c].reshape(twice, hid), spread, (((0,), (0,)), ((), ())), preferred_element_type=f32
        ).astype(bf16)

        @pl.when(c == 0)
        def _():
            for v in range(2):
                wd[v] = piece[:, v * wide:(v + 1) * wide]

        @pl.when(c > 0)
        def _():
            for v in range(2):
                wd[v] = wd[v] + piece[:, v * wide:(v + 1) * wide]

    def dispatch(s):
        weights = agw[:, s].reshape(line, experts)
        named = (weights > 0).astype(f32)
        ahead = mm(lower, named.astype(bf16))
        turn = (named * (ahead + 1.0)).astype(bf16)
        chosen = (mm_nt(pick, turn) == order_col) & spot
        ring_end(s)
        moved = mm(chosen.astype(f32).astype(bf16), ag[s].reshape(line, width))
        xs[s] = moved.astype(bf16).reshape(nx, nz, slots, width)
        for dx in range(1, nx):
            send(xs.at[s, dx], x1.at[s, dx], s_x, r_x.at[s], x_peer(dx))
        x1[s, 0] = xs[s, 0]
        kept = (mm_nt(turn, pick_back) == order_row) & spot_t
        upper = weights.astype(bf16)
        lesser = (weights - upper.astype(f32)).astype(bf16)
        cmb[s, 0] = jnp.where(kept, mm_nt(upper, pick_back), 0.0).astype(bf16)
        cmb[s, 1] = jnp.where(kept, mm_nt(lesser, pick_back), 0.0).astype(bf16)

    def relay(s):
        await_bytes(x1.at[s, rest_x], r_x.at[s])
        for dz in range(1, nz):
            send(x1.at[s, :, dz], xr.at[s, dz], s_z, r_z.at[s], ring_peer(dz, 1))
        xr[s, 0] = x1[s, :, 0]

    def expert_in(s):
        await_bytes(xr.at[s, rest_z], r_z.at[s])
        items = xr[s].reshape(nq * slots, width)
        part[s, 0] = mm(items, gate_up[0])
        part[s, 1] = mm(items, gate_up[1])
        send(part.at[s], partr.at[s], s_grp, r_grp.at[s], grp_mate)

    def expert_mid(s):
        await_bytes(partr.at[s], r_grp.at[s])
        gated = part[s, 0] + partr[s, 0]
        upped = part[s, 1] + partr[s, 1]
        hd[s] = (gated / (1.0 + jnp.exp(-gated)) * upped).astype(bf16)

    def expert_out(s, carry):
        for v in range(2):
            u = 2 * s + v
            ys[u] = mm(hd[s], wd[v]).astype(bf16).reshape(nz, nx, slots, wide)
            for dx in range(1, nx):
                send(ys.at[u, :, dx], x2.at[u, dx], s_rx, r_rx.at[u], x_peer(-dx))
            x2[u, 0] = ys[u, :, 0]
        return carry

    def relay_back(u):
        await_bytes(x2.at[u, rest_x], r_rx.at[u])
        for dz in range(1, nz):
            send(x2.at[u, :, dz], yr.at[u, dz], s_rz, r_rz.at[u], ring_peer(dz, -1))
        yr[u, 0] = x2[u, :, 0]

    def combine(u):
        await_bytes(yr.at[u, rest_z], r_rz.at[u])
        items = yr[u].reshape(nq * slots, wide)
        s = u // 2
        mixed = mm(cmb[s, 0], items) + mm(cmb[s, 1], items)
        rs[u] = mixed.astype(bf16).reshape(ny, rows, wide)
        for dy in range(1, ny):
            send(rs.at[u, dy], rr.at[u, dy], s_rs, r_rs.at[u], y_peer(-dy))
        rr[u, 0] = rs[u, 0]

    def total(u):
        await_bytes(rr.at[u, rest_y], r_rs.at[u])
        mixed = rr[u, 0].astype(f32)
        for dy in range(1, ny):
            mixed += rr[u, dy].astype(f32)
        ts[u] = mixed.astype(bf16)
        send(ts.at[u], tr.at[u], s_tp, r_tp.at[u], tp_mate)

    def finish(u):
        await_bytes(tr.at[u], r_tp.at[u])
        at = pl.ds(pl.multiple_of((u % 2) * wide, wide), wide)
        out[u // 2, :, at] = (ts[u].astype(f32) + tr[u].astype(f32)).astype(bf16)

    def staged(i, plan, upto):
        for stage, lag in plan:
            @pl.when((i >= lag) & (i < lag + upto))
            def _():
                stage(i - lag)

    await_bytes(nmr.at[rest_y], r_nm)
    index_e = iota((experts, experts), 0).astype(f32)

    def spread_weights(dy, carry):
        names, shares = nmr[dy, 0], nmr[dy, 1]
        weight_of = jnp.zeros((experts, experts), f32)
        for k in range(top):
            weight_of += jnp.where(names[k:k + 1, :] == index_e, shares[k:k + 1, :], 0.0)
        agw[dy] = weight_of.T[:count].reshape(steps, rows, experts)
        return carry

    lax.fori_loop(0, ny, spread_weights, 0)

    def forth(i, carry):
        staged(i, [(dispatch, 0), (code_z, -2), (code_y, 0), (relay, 1), (place, 2), (expert_mid, 4)], steps)
        first = jnp.where(i < 6, 0, i - 4)
        lax.fori_loop(first, jnp.where(i < 5, 0, i - 3), expert_out, 0)
        staged(i, [(expert_in, 3)], steps)
        return carry

    def back(i, carry):
        staged(i, [(relay_back, 0), (combine, 2), (total, 4), (finish, 6)], 2 * steps)
        return carry

    lax.fori_loop(0, steps + 4, forth, 0)
    lax.fori_loop(0, 2 * steps + 6, back, 0)

    await_bytes(nmr.at[rest_y], s_nm)
    await_bytes(ag.at[:, rest_y], s_ag)
    await_bytes(pkr.at[rest_y], s_pk)
    await_bytes(pk2r, s_pk2)
    await_bytes(c1.at[:, rest_x], s_cx)
    await_bytes(c2.at[:, rest_z], s_cz)
    await_bytes(rb.at[:, rest_y], s_cy)
    await_bytes(x1.at[:, rest_x], s_x)
    await_bytes(xr.at[:, rest_z], s_z)
    await_bytes(partr, s_grp)
    await_bytes(x2.at[:, rest_x], s_rx)
    await_bytes(yr.at[:, rest_z], s_rz)
    await_bytes(rr.at[:, rest_y], s_rs)
    await_bytes(tr, s_tp)


def on_device(nz, nx, ny, master, gate_up, owner_map, tokens, routes, gate_weights):
    steps, rows, width = tokens.shape
    depth, experts, hid = master.shape
    top_rows = routes.shape[2]
    parts = depth // 2
    nq = nz * nx
    slots = 2 * ny
    line = ny * rows
    vmem = pltpu.VMEM
    dma = pltpu.SemaphoreType.DMA
    wide = width // 2
    by_x = vmem((steps, nx, nz, slots, width), bf16)
    by_z = vmem((steps, nz, nx, slots, width), bf16)
    back_x = vmem((2 * steps, nx, nz, slots, wide), bf16)
    back_z = vmem((2 * steps, nz, nx, slots, wide), bf16)
    back_y = vmem((2 * steps, ny, rows, wide), bf16)
    back_own = vmem((2 * steps, rows, wide), bf16)
    sums = vmem((steps, 2, nq * slots, hid), f32)
    named = vmem((2, top_rows, experts), f32)
    peak = vmem((8, experts), f32)
    code_x = vmem((parts, nx, nz, slots, hid), bf16)
    code_z = vmem((parts, nz, nx, slots, hid), bf16)
    code_y = vmem((parts, ny, 2 * nq, hid), bf16)
    scratch = [
        named, vmem((ny, 2, top_rows, experts), f32),
        vmem((ny, steps, rows, experts), f32),
        vmem((steps, ny, rows, width), bf16),
        by_x, by_x, by_z,
        vmem((steps, 2, line, nq * slots), bf16),
        sums, sums,
        vmem((steps, nq * slots, hid), bf16),
        back_z, back_x, back_z, back_y, back_y, back_own, back_own,
        peak, vmem((ny, 8, experts), f32), peak, peak,
        code_x, code_x, code_z, code_y, code_y,
        vmem((2, hid, wide), bf16),
    ]
    per_step, per_part, per_half = dma((steps,)), dma((parts,)), dma((2 * steps,))
    scratch += [dma] * 14
    scratch += [
        dma((steps, ny)), dma, per_step, per_step, per_step, per_half, per_half, per_half, per_half,
        dma, dma, per_part, per_part, per_part,
    ]
    return pl.pallas_call(
        functools.partial(kernel, nz, nx, ny),
        out_shape=jax.ShapeDtypeStruct((steps, rows, width), bf16),
        in_specs=[pl.BlockSpec(memory_space=vmem)] * 6,
        out_specs=pl.BlockSpec(memory_space=vmem),
        scratch_shapes=scratch,
        compiler_params=pltpu.CompilerParams(
            collective_id=0, has_side_effects=True, vmem_limit_bytes=56 * 2**20
        ),
    )(
        master,
        gate_up[0],
        owner_map.reshape(1, experts),
        tokens,
        jnp.swapaxes(routes, 1, 2),
        jnp.swapaxes(gate_weights, 1, 2),
    )


def solution(mesh, sizes=(4, 4, 8)):
    placed = (
        P(("grp", "ep"), None, "tp"),
        P("ep", None, "grp", "tp"),
        P(),
        P(None, "ep", "grp"),
        P(None, "ep", None),
        P(None, "ep", None),
    )
    return jax.shard_map(
        functools.partial(on_device, *sizes),
        mesh=mesh, in_specs=placed, out_specs=P(None, "ep", "grp"), check_vma=False,
    )
```

```python
import functools

import jax
import jax.numpy as jnp
from jax import lax
from jax.experimental import pallas as pl
from jax.experimental.pallas import tpu as pltpu
from jax.sharding import PartitionSpec as P

f32 = jnp.float32
bf16 = jnp.bfloat16
NT = (((1,), (1,)), ((), ()))


def mm(a, b):
    return jnp.dot(a, b, preferred_element_type=f32)


def mm_nt(a, b):
    return lax.dot_general(a, b, NT, preferred_element_type=f32)


def iota(shape, dim):
    return lax.broadcasted_iota(jnp.int32, shape, dim)


def snap(values):
    magnitude = jnp.abs(values)
    magnitude = magnitude + magnitude * 2.0 ** (-22)
    large = magnitude * (2.0**20 + 1.0)
    fine = large - (large - magnitude)
    coarse = (magnitude + 24576.0) - 24576.0
    snapped = jnp.where(magnitude < 2.0 ** (-5), coarse, fine)
    return jnp.where(values < 0, -snapped, snapped)


def kernel(
    nz, nx, ny,
    master_in, gate_up_in, owner_map, tokens, routes, gates,
    out, master, gate_up,
    nm, nmr, agw, ag, xs, x1, xr, cmb, part, partr, hd, ys, x2, yr, rs, rr, ts, tr,
    pk, pkr, pk2, pk2r, sa, c1, c2, sb, rb, wd,
    s_ag, s_nm, s_x, s_z, s_grp, s_rz, s_rx, s_rs, s_tp, s_pk, s_pk2, s_cx, s_cz, s_cy,
    in_m, in_g, r_ag, r_nm, r_x, r_z, r_grp, r_rz, r_rx, r_rs, r_tp, r_pk, r_pk2, r_cx, r_cz, r_cy,
):
    steps, rows, width = tokens.shape
    experts = owner_map.shape[1]
    top = routes.shape[1]
    depth, _, hid = master.shape
    parts = depth // 2
    nq = nz * nx
    slots = 2 * ny
    line = ny * rows
    wide = width // 2
    g = lax.axis_index("grp")
    ep = lax.axis_index("ep")
    t = lax.axis_index("tp")
    z, x, y = ep // (nx * ny), (ep // ny) % nx, ep % ny
    zz = t * nz + z

    def y_peer(dy):
        return {"ep": ep - y + (y + dy + ny) % ny}

    def x_peer(dx):
        return {"ep": ep + ((x + dx + nx) % nx - x) * ny}

    def ring_peer(dz, sign):
        if 2 * dz < nz:
            off = dz
        elif 2 * dz > nz:
            off = dz - nz
        else:
            off = dz * (1 - 2 * g)
        zt = (zz + sign * off + 2 * nz) % (2 * nz)
        return {"ep": ep + (zt % nz - z) * (nx * ny), "tp": zt // nz}

    def group_peer(dz):
        return {"ep": ep + ((z + dz) % nz - z) * (nx * ny)}

    x_mate = {"ep": ep + (1 - 2 * (x % 2)) * ny}
    grp_mate = {"grp": 1 - g}
    tp_mate = {"tp": 1 - t}

    greeted = [y_peer(dy) for dy in range(1, ny)]
    greeted += [x_peer(dx) for dx in range(1, nx)]
    greeted += [ring_peer(dz, 1) for dz in range(1, nz)]
    greeted += [ring_peer(nz // 2, -1)]
    greeted += [group_peer(dz) for dz in range(1, nz)]
    greeted += [grp_mate, tp_mate]
    barrier = pltpu.get_barrier_semaphore()
    for peer in greeted:
        pl.semaphore_signal(barrier, inc=1, device_id=peer, device_id_type=pl.DeviceIdType.MESH)

    load_m = pltpu.make_async_copy(master_in, master, in_m)
    load_g = pltpu.make_async_copy(gate_up_in, gate_up, in_g)
    load_m.start()
    load_g.start()

    def send(src, dst, ssem, rsem, peer):
        pltpu.make_async_remote_copy(
            src_ref=src, dst_ref=dst, send_sem=ssem, recv_sem=rsem,
            device_id=peer, device_id_type=pl.DeviceIdType.MESH,
        ).start()

    def await_bytes(ref, sem):
        pltpu.make_async_copy(ref, ref, sem).wait()

    rest_x, rest_y, rest_z = pl.ds(1, nx - 1), pl.ds(1, ny - 1), pl.ds(1, nz - 1)

    load_m.wait()
    cols = hid // 128
    lanes_p = iota((experts, 128), 1)
    peaks = jnp.zeros((experts, 128), f32)
    for j in range(cols):
        most = jnp.abs(master[0, :, j * 128:(j + 1) * 128])
        for d in range(1, depth):
            most = jnp.maximum(most, jnp.abs(master[d, :, j * 128:(j + 1) * 128]))
        peaks = jnp.where(lanes_p == j, jnp.max(most, axis=1, keepdims=True), peaks)
    pk[...] = peaks.T[:8]
    pkr[0] = pk[...]
    ag[:, 0] = tokens[...]

    count = steps * rows
    blank = [jnp.zeros((top, experts - count), f32)]
    nm[0] = jnp.concatenate([routes[s].astype(f32) for s in range(steps)] + blank, axis=1)
    nm[1] = jnp.concatenate([gates[s] for s in range(steps)] + blank, axis=1)
    nmr[0] = nm[...]
    pl.semaphore_wait(barrier, len(greeted))

    for dy in range(1, ny):
        send(pk, pkr.at[dy], s_pk, r_pk, y_peer(dy))
    for dy in range(1, ny):
        send(nm, nmr.at[dy], s_nm, r_nm, y_peer(dy))

    def hop(s, h, sign):
        held = (h - 1) * sign % ny
        if h > 1:
            await_bytes(ag.at[s, held], r_ag.at[s, held])
        place_at = h * sign % ny
        send(ag.at[s, held], ag.at[s, place_at], s_ag, r_ag.at[s, place_at], y_peer(sign))

    def ring(h):
        if 2 * h < ny:
            def both_ways(s, carry):
                hop(s, h, 1)
                hop(s, h, -1)
                return carry

            lax.fori_loop(0, steps, both_ways, 0)
        else:
            for s in range(steps):
                hop(s, h, 1 - 2 * (s % 2))

    def ring_end(s):
        await_bytes(ag.at[s, ny // 2], r_ag.at[s, ny // 2])
        last = ny // 2 + 1 - 2 * (s % 2)
        await_bytes(ag.at[s, last], r_ag.at[s, last])

    ring(1)
    await_bytes(pkr.at[rest_y], r_pk)
    pk2[...] = jnp.max(pkr[...], axis=0)
    send(pk2, pk2r, s_pk2, r_pk2, x_mate)
    ring(2)

    row_q = iota((nq * slots, 1), 0)
    peer_q = row_q // slots
    owner_q = (
        ((z + peer_q % nz) % nz) * (nx * ny) + ((x + peer_q // nz) % nx) * ny + y
    )
    pick = (owner_map[...] == owner_q).astype(f32).astype(bf16)
    owner_b = (
        ((z + peer_q // nx) % nz) * (nx * ny) + ((x + peer_q % nx) % nx) * ny + y
    )
    pick_back = (owner_map[...] == owner_b).astype(f32).astype(bf16)
    slot_col = row_q % slots
    slot_row = iota((1, nq * slots), 1) % slots
    row_col = iota((line, 1), 0) // rows
    row_row = iota((1, line), 1) // rows
    la, lb = iota((line, line), 0), iota((line, line), 1)
    lower = ((la // rows == lb // rows) & (lb < la)).astype(f32).astype(bf16)
    spot = ((slot_col // 2) == row_row)
    spot_t = ((slot_row // 2) == row_col)
    order_col = (slot_col % 2 + 1).astype(f32)
    order_row = (slot_row % 2 + 1).astype(f32)

    twice = 2 * experts
    row_p = iota((twice, 1), 0)
    owner_p = (
        ((z + (row_p // slots) % nz) % nz) * (nx * ny)
        + ((x + row_p // (slots * nz)) % nx) * ny
        + (y + (row_p // 2) % ny) % ny
    )
    owner_two = jnp.concatenate([owner_map[...], owner_map[...]], axis=1)
    half_two = iota((1, twice), 1) // experts
    order_p = ((owner_two == owner_p) & (half_two == row_p % 2)).astype(f32).astype(bf16)

    await_bytes(pk2r, r_pk2)
    both = jnp.maximum(pk2[...], pk2r[...])
    scale_t = (both + 1e-06) / 448.0
    scale = jnp.concatenate([scale_t, jnp.ones((128 - 8, experts), f32)], axis=0).T
    inverse = 1.0 / scale

    def code(c, carry):
        halves = []
        for h in range(2):
            pieces = []
            for j in range(cols):
                field = master[h * parts + c, :, j * 128:(j + 1) * 128]
                pieces.append((snap(field * inverse[:, j:j + 1]) * scale[:, j:j + 1]).astype(bf16))
            halves.append(jnp.concatenate(pieces, axis=1))
        moved = mm(order_p, jnp.concatenate(halves, axis=0))
        moved = moved.astype(bf16).reshape(nx, nz, slots, hid)
        sa[c] = moved
        for dx in range(1, nx):
            send(sa.at[c, dx], c1.at[c, dx], s_cx, r_cx.at[c], x_peer(dx))
        c1[c, 0] = sa[c, 0]
        return carry

    def code_z(c):
        await_bytes(c1.at[c, rest_x], r_cx.at[c])
        for dz in range(1, nz):
            send(c1.at[c, :, dz], c2.at[c, dz], s_cz, r_cz.at[c], group_peer(dz))
        c2[c, 0] = c1[c, :, 0]

    code(0, 0)
    ring(3)
    code(1, 0)
    code_z(0)
    for h in range(4, ny // 2 + 1):
        ring(h)
    code(2, 0)
    code_z(1)
    code(3, 0)

    ra_, rb_ = iota((twice, 1), 0), iota((1, twice), 1)
    per_y = 2 * nq
    regroup = (
        rb_ == ((ra_ % per_y) // 2) * slots + (ra_ // per_y) * 2 + ra_ % 2
    ).astype(f32).astype(bf16)

    def code_y(c):
        await_bytes(c2.at[c, rest_z], r_cz.at[c])
        moved = mm(regroup, c2[c].reshape(twice, hid)).astype(bf16).reshape(ny, per_y, hid)
        sb[c] = moved
        for dy in range(1, ny):
            send(sb.at[c, dy], rb.at[c, dy], s_cy, r_cy.at[c], y_peer(dy))
        rb[c, 0] = sb[c, 0]

    row_r = iota((twice, 1), 0)
    source_r = (
        ((z - row_r // (2 * nx) % nz + nz) % nz) * (nx * ny)
        + ((x - (row_r // 2) % nx + nx) % nx) * ny
        + (y - row_r // per_y + ny) % ny
    )
    base_r = source_r * depth + (row_r % 2) * parts
    feature = iota((1, width), 1)

    def place(c):
        await_bytes(rb.at[c, rest_y], r_cy.at[c])
        spread = (feature == base_r + c).astype(f32).astype(bf16)
        piece = lax.dot_general(
            rb[c].reshape(twice, hid), spread, (((0,), (0,)), ((), ())), preferred_element_type=f32
        ).astype(bf16)

        @pl.when(c == 0)
        def _():
            for v in range(2):
                wd[v] = piece[:, v * wide:(v + 1) * wide]

        @pl.when(c > 0)
        def _():
            for v in range(2):
                wd[v] = wd[v] + piece[:, v * wide:(v + 1) * wide]

    def dispatch(s):
        weights = agw[:, s].reshape(line, experts)
        named = (weights > 0).astype(f32)
        ahead = mm(lower, named.astype(bf16))
        turn = (named * (ahead + 1.0)).astype(bf16)
        chosen = (mm_nt(pick, turn) == order_col) & spot
        ring_end(s)
        moved = mm(chosen.astype(f32).astype(bf16), ag[s].reshape(line, width))
        xs[s] = moved.astype(bf16).reshape(nx, nz, slots, width)
        for dx in range(1, nx):
            send(xs.at[s, dx], x1.at[s, dx], s_x, r_x.at[s], x_peer(dx))
        x1[s, 0] = xs[s, 0]
        kept = (mm_nt(turn, pick_back) == order_row) & spot_t
        upper = weights.astype(bf16)
        lesser = (weights - upper.astype(f32)).astype(bf16)
        cmb[s, 0] = jnp.where(kept, mm_nt(upper, pick_back), 0.0).astype(bf16)
        cmb[s, 1] = jnp.where(kept, mm_nt(lesser, pick_back), 0.0).astype(bf16)

    def relay(s):
        await_bytes(x1.at[s, rest_x], r_x.at[s])
        for dz in range(1, nz):
            send(x1.at[s, :, dz], xr.at[s, dz], s_z, r_z.at[s], ring_peer(dz, 1))
        xr[s, 0] = x1[s, :, 0]

    def expert_in(s):
        await_bytes(xr.at[s, rest_z], r_z.at[s])
        items = xr[s].reshape(nq * slots, width)
        part[s, 0] = mm(items, gate_up[0])
        part[s, 1] = mm(items, gate_up[1])
        send(part.at[s], partr.at[s], s_grp, r_grp.at[s], grp_mate)

    def expert_mid(s):
        await_bytes(partr.at[s], r_grp.at[s])
        gated = part[s, 0] + partr[s, 0]
        upped = part[s, 1] + partr[s, 1]
        hd[s] = (gated / (1.0 + jnp.exp(-gated)) * upped).astype(bf16)

    def expert_out(s, carry):
        for v in range(2):
            u = 2 * s + v
            ys[u] = mm(hd[s], wd[v]).astype(bf16).reshape(nz, nx, slots, wide)
            for dx in range(1, nx):
                send(ys.at[u, :, dx], x2.at[u, dx], s_rx, r_rx.at[u], x_peer(-dx))
            x2[u, 0] = ys[u, :, 0]
        return carry

    def relay_back(u):
        await_bytes(x2.at[u, rest_x], r_rx.at[u])
        for dz in range(1, nz):
            send(x2.at[u, :, dz], yr.at[u, dz], s_rz, r_rz.at[u], ring_peer(dz, -1))
        yr[u, 0] = x2[u, :, 0]

    def combine(u):
        await_bytes(yr.at[u, rest_z], r_rz.at[u])
        items = yr[u].reshape(nq * slots, wide)
        s = u // 2
        mixed = mm(cmb[s, 0], items) + mm(cmb[s, 1], items)
        rs[u] = mixed.astype(bf16).reshape(ny, rows, wide)
        for dy in range(1, ny):
            send(rs.at[u, dy], rr.at[u, dy], s_rs, r_rs.at[u], y_peer(-dy))
        rr[u, 0] = rs[u, 0]

    def total(u):
        await_bytes(rr.at[u, rest_y], r_rs.at[u])
        mixed = rr[u, 0].astype(f32)
        for dy in range(1, ny):
            mixed += rr[u, dy].astype(f32)
        ts[u] = mixed.astype(bf16)
        send(ts.at[u], tr.at[u], s_tp, r_tp.at[u], tp_mate)

    def finish(u):
        await_bytes(tr.at[u], r_tp.at[u])
        at = pl.ds(pl.multiple_of((u % 2) * wide, wide), wide)
        out[u // 2, :, at] = (ts[u].astype(f32) + tr[u].astype(f32)).astype(bf16)

    def staged(i, plan, upto):
        for stage, lag in plan:
            @pl.when((i >= lag) & (i < lag + upto))
            def _():
                stage(i - lag)

    await_bytes(nmr.at[rest_y], r_nm)
    index_e = iota((experts, experts), 0).astype(f32)

    def spread_weights(dy, carry):
        names, shares = nmr[dy, 0], nmr[dy, 1]
        weight_of = jnp.zeros((experts, experts), f32)
        for k in range(top):
            weight_of += jnp.where(names[k:k + 1, :] == index_e, shares[k:k + 1, :], 0.0)
        agw[dy] = weight_of.T[:count].reshape(steps, rows, experts)
        return carry

    lax.fori_loop(0, ny, spread_weights, 0)

    def forth(i, carry):
        staged(i, [(dispatch, 0), (code_z, -2), (code_y, 0), (relay, 1), (place, 2), (expert_mid, 4)], steps)
        first = jnp.where(i < 6, 0, i - 4)
        lax.fori_loop(first, jnp.where(i < 5, 0, i - 3), expert_out, 0)
        staged(i, [(expert_in, 3)], steps)
        return carry

    def back(i, carry):
        staged(i, [(relay_back, 0), (combine, 3), (total, 6), (finish, 8)], 2 * steps)
        return carry

    load_g.wait()
    lax.fori_loop(0, steps + 4, forth, 0)
    lax.fori_loop(0, 2 * steps + 8, back, 0)

    await_bytes(nmr.at[rest_y], s_nm)
    await_bytes(ag.at[:, rest_y], s_ag)
    await_bytes(pkr.at[rest_y], s_pk)
    await_bytes(pk2r, s_pk2)
    await_bytes(c1.at[:, rest_x], s_cx)
    await_bytes(c2.at[:, rest_z], s_cz)
    await_bytes(rb.at[:, rest_y], s_cy)
    await_bytes(x1.at[:, rest_x], s_x)
    await_bytes(xr.at[:, rest_z], s_z)
    await_bytes(partr, s_grp)
    await_bytes(x2.at[:, rest_x], s_rx)
    await_bytes(yr.at[:, rest_z], s_rz)
    await_bytes(rr.at[:, rest_y], s_rs)
    await_bytes(tr, s_tp)


def on_device(nz, nx, ny, master, gate_up, owner_map, tokens, routes, gate_weights):
    steps, rows, width = tokens.shape
    depth, experts, hid = master.shape
    top_rows = routes.shape[2]
    parts = depth // 2
    nq = nz * nx
    slots = 2 * ny
    line = ny * rows
    vmem = pltpu.VMEM
    dma = pltpu.SemaphoreType.DMA
    wide = width // 2
    by_x = vmem((steps, nx, nz, slots, width), bf16)
    by_z = vmem((steps, nz, nx, slots, width), bf16)
    back_x = vmem((2 * steps, nx, nz, slots, wide), bf16)
    back_z = vmem((2 * steps, nz, nx, slots, wide), bf16)
    back_y = vmem((2 * steps, ny, rows, wide), bf16)
    back_own = vmem((2 * steps, rows, wide), bf16)
    sums = vmem((steps, 2, nq * slots, hid), f32)
    named = vmem((2, top_rows, experts), f32)
    peak = vmem((8, experts), f32)
    code_x = vmem((parts, nx, nz, slots, hid), bf16)
    code_z = vmem((parts, nz, nx, slots, hid), bf16)
    code_y = vmem((parts, ny, 2 * nq, hid), bf16)
    scratch = [
        vmem(master.shape, f32), vmem(gate_up.shape[1:], bf16),
        named, vmem((ny, 2, top_rows, experts), f32),
        vmem((ny, steps, rows, experts), f32),
        vmem((steps, ny, rows, width), bf16),
        by_x, by_x, by_z,
        vmem((steps, 2, line, nq * slots), bf16),
        sums, sums,
        vmem((steps, nq * slots, hid), bf16),
        back_z, back_x, back_z, back_y, back_y, back_own, back_own,
        peak, vmem((ny, 8, experts), f32), peak, peak,
        code_x, code_x, code_z, code_y, code_y,
        vmem((2, hid, wide), bf16),
    ]
    per_step, per_part, per_half = dma((steps,)), dma((parts,)), dma((2 * steps,))
    scratch += [dma] * 16
    scratch += [
        dma((steps, ny)), dma, per_step, per_step, per_step, per_half, per_half, per_half, per_half,
        dma, dma, per_part, per_part, per_part,
    ]
    return pl.pallas_call(
        functools.partial(kernel, nz, nx, ny),
        out_shape=jax.ShapeDtypeStruct((steps, rows, width), bf16),
        in_specs=[pl.BlockSpec(memory_space=pl.ANY)] * 2 + [pl.BlockSpec(memory_space=vmem)] * 4,
        out_specs=pl.BlockSpec(memory_space=vmem),
        scratch_shapes=scratch,
        compiler_params=pltpu.CompilerParams(
            collective_id=0, has_side_effects=True, vmem_limit_bytes=56 * 2**20
        ),
    )(
        master,
        gate_up[0],
        owner_map.reshape(1, experts),
        tokens,
        jnp.swapaxes(routes, 1, 2),
        jnp.swapaxes(gate_weights, 1, 2),
    )


def solution(mesh, sizes=(4, 4, 8)):
    placed = (
        P(("grp", "ep"), None, "tp"),
        P("ep", None, "grp", "tp"),
        P(),
        P(None, "ep", "grp"),
        P(None, "ep", None),
        P(None, "ep", None),
    )
    return jax.shard_map(
        functools.partial(on_device, *sizes),
        mesh=mesh, in_specs=placed, out_specs=P(None, "ep", "grp"), check_vma=False,
    )
```
